256 devices in a mesh: ctx: 16 (over z_lo, x), tp: 16 (over z_hi, y, core).
Axes of the slice: x: 4, y: 4, z: 8 (z_hi: 2, z_lo: 4; z = z_hi * 4 + z_lo), core: 2. Of those that a mesh axis runs over, the one named last changes fastest.
Arguments:
- hidden_in: bfloat16 [4096, 4096], P('tp', 'ctx'), may hold values from -24 to 24
- norm_gain: float32 [4096], replicated, may hold values from 0.1 to 1.9
- in_weight: bfloat16 [3, 4096, 4096], P(None, 'tp'), may hold values from -0.125 to 0.125
- filters: float32 [256, 128], P('tp'), may hold values from -0.5 to 0.5
- out_weight: bfloat16 [4096, 4096], P('tp'), may hold values from -0.125 to 0.125
- out_grads: bfloat16 [4096, 4096], P('tp', 'ctx'), may hold values from -6 to 6
Outputs:
- layer_out: bfloat16 [4096, 4096], P('tp', 'ctx')
- hidden_grads: bfloat16 [4096, 4096], P('tp', 'ctx')
- in_weight_grads: float32 [3, 4096, 4096], P(None, 'tp', 'ctx')
- filter_grads: float32 [256, 128], P(('tp', 'ctx'))
- out_weight_grads: float32 [4096, 4096], P('tp', 'ctx')
The draws below stay inside these ranges and needn't reach their ends.
All inputs are finite; a program needn't handle non-finite values.
Results may differ from the reference program's by a relative error of at most 0.03.
Values may be sent and summed in bfloat16 or wider, within the bound.
No kernel may reach another device: no remote copies, remote signals or barrier semaphores. Data moves between devices by JAX's collectives and lax.ppermute only.
A program may use at most 128 MiB of HBM per device.

```python
import jax
import jax.numpy as jnp
from jax import lax

D = 4096
GS = 16
TAPS = 128
TOK_DEV = 256
L = 4096
GROUPS = 256
N_CTX = 16
N_TP = 16


def draw_hidden_in(key, part):
    key = jax.random.fold_in(key, 11)
    values = jnp.clip(jax.random.normal(key, (D, L), jnp.float32), -6.0, 6.0)
    rising = jnp.exp(jnp.linspace(jnp.log(0.5), jnp.log(4.0), D)).astype(jnp.float32)
    return (values * rising[:, None]).astype(jnp.bfloat16)


def spiked(array, own_key, source, target, blocks, factor):
    owner, partner = [(jnp.arange(array.shape[axis_at]) // (array.shape[axis_at] // blocks)).reshape([-1 if axis == axis_at else 1 for axis in range(array.ndim)]) for axis_at in (source, target)]
    chosen = jax.random.permutation(own_key, blocks)[partner]
    strong = (owner == chosen) | (owner == (partner + blocks // 2) % blocks)
    return jnp.where(strong, factor * array, array)


def steps_of(own_key, dims, cuts, least, high):
    def one(position, shards_of):
        draws = jax.random.uniform(jax.random.fold_in(jax.random.fold_in(own_key, 6), position), (shards_of,), jnp.float32, least / len(cuts), high / len(cuts))
        return jnp.repeat(jnp.exp(draws), dims[position] // shards_of).reshape((-1,) + (1,) * (len(dims) - position - 1))

    level = one(*cuts[0])
    for cut in cuts[1:]:
        level = level * one(*cut)
    return level


def bell_draw(key, dims, scale, limit, split=(), dtype=jnp.bfloat16):
    values = jax.random.normal(key, dims, jnp.float32) * scale
    if len(split) > 0:
        values = steps_of(key, dims, split, -0.22, 0.18) * values
    return jnp.clip(values, min=-limit, max=limit).astype(dtype)


def gaussian_with(own_key, shape, deviation, reach, cuts, heavy, dtype=jnp.bfloat16):
    result = deviation * jax.random.normal(own_key, shape, jnp.float32)
    if cuts:
        result = result * steps_of(own_key, shape, cuts, -0.22, 0.18)
    return jnp.clip(spiked(result, jax.random.fold_in(own_key, 3), *heavy), -reach, reach).astype(dtype)


def setup_inputs(seed: int = 0) -> dict:
    splits = jax.random.split(jax.random.key(seed), 7)
    return {
        "hidden_in": draw_hidden_in(jax.random.fold_in(splits[6], 71), 0),
        "norm_gain": jnp.clip(1.0 + 0.18 * jax.random.normal(splits[1], (D,), jnp.float32), 0.1, 1.9),
        "in_weight": gaussian_with(splits[2], (3, D, D), D ** -0.5, 0.125, ((1, 16),), (1, 2, 16, 2.0)),
        "filters": bell_draw(splits[3], (GROUPS, TAPS), TAPS ** -0.5, 0.5, ((0, 16),), jnp.float32),
        "out_weight": gaussian_with(splits[4], (D, D), D ** -0.5, 0.125, ((0, 16),), (0, 1, 16, 2.0)),
        "out_grads": bell_draw(splits[5], (D, L), 1.0, 6.0, ((0, 16), (1, 16))),
    }


EPS = 1e-06
HIGH = lax.Precision.HIGHEST

def lag_tables(tap_count):
    lag_index = jnp.arange(tap_count)
    offsets = lag_index[None, :] - lag_index[:, None]
    same_sel = (offsets[None, :, :] == lag_index[:, None, None]).astype(jnp.float32)
    prev_sel = (offsets[None, :, :] + tap_count == lag_index[:, None, None]).astype(jnp.float32)
    return (same_sel, prev_sel)

def toeplitz(narrow_filters, same_sel, prev_sel):
    wide = narrow_filters.astype(jnp.float32)
    same_block = jnp.einsum('gk,kst->gst', wide, same_sel, precision=HIGH)
    prev_block = jnp.einsum('gk,kst->gst', wide, prev_sel, precision=HIGH)
    return (same_block, prev_block)

def ctx_partials(left_data, right_data):

    def add_block(index, total):
        first_tok = (index * TOK_DEV).astype(jnp.int32)
        left_part = lax.dynamic_slice_in_dim(left_data, first_tok, TOK_DEV, 2).astype(jnp.float32)
        right_part = lax.dynamic_slice_in_dim(right_data, first_tok, TOK_DEV, 1).astype(jnp.float32)
        term = jnp.einsum('pot,it->poi', left_part, right_part, precision=HIGH)
        rounded = lax.optimization_barrier(term.astype(jnp.bfloat16))
        return total + rounded.astype(jnp.float32)
    start_total = jnp.zeros((left_data.shape[0], left_data.shape[1], right_data.shape[0]), jnp.float32)
    return lax.fori_loop(0, N_CTX, add_block, start_total)

def reference(hidden_in, norm_gain, in_weight, filters, out_weight, out_grads):
    hidden_f = hidden_in.astype(jnp.float32)
    rms_scale = lax.rsqrt(lax.optimization_barrier(jnp.mean(hidden_f * hidden_f, axis=0)) + EPS)
    normed = (hidden_f * rms_scale[None, :] * norm_gain[:, None]).astype(jnp.bfloat16)
    query_part = jnp.dot(in_weight[0], normed, preferred_element_type=jnp.float32).astype(jnp.bfloat16)
    key_part = jnp.dot(in_weight[1], normed, preferred_element_type=jnp.float32).astype(jnp.bfloat16)
    value_part = jnp.dot(in_weight[2], normed, preferred_element_type=jnp.float32).astype(jnp.bfloat16)
    mixed_in = (key_part.astype(jnp.float32) * value_part.astype(jnp.float32)).astype(jnp.bfloat16)
    same_sel, prev_sel = lag_tables(TAPS)
    same_block, prev_block = toeplitz(filters.astype(jnp.bfloat16), same_sel, prev_sel)
    blocks = mixed_in.astype(jnp.float32).reshape(GROUPS, GS, L // TAPS, TAPS)
    before = jnp.concatenate([jnp.zeros_like(blocks[:, :, :1]), blocks[:, :, :-1]], axis=2)
    convolved = jnp.einsum('gcnb,gbt->gcnt', blocks, same_block, precision=HIGH) + jnp.einsum('gcnb,gbt->gcnt', before, prev_block, precision=HIGH)
    convolved = convolved.reshape(D, L).astype(jnp.bfloat16)
    mixed = (query_part.astype(jnp.float32) * convolved.astype(jnp.float32)).astype(jnp.bfloat16)
    layer_out = (hidden_f + jnp.dot(out_weight, mixed, preferred_element_type=jnp.float32)).astype(jnp.bfloat16)
    out_weight_grads = ctx_partials(out_grads[None], mixed)[0]
    width_tp = D // N_TP

    def add_tp_block(index, total):
        first_row = (index * width_tp).astype(jnp.int32)
        weight_rows = lax.dynamic_slice_in_dim(out_weight, first_row, width_tp, 0)
        grad_rows = lax.dynamic_slice_in_dim(out_grads, first_row, width_tp, 0)
        term = jnp.dot(weight_rows.T, grad_rows, preferred_element_type=jnp.float32)
        rounded = lax.optimization_barrier(term.astype(jnp.bfloat16))
        return total + rounded.astype(jnp.float32)
    mixed_grads = lax.fori_loop(0, N_TP, add_tp_block, jnp.zeros((D, L), jnp.float32)).astype(jnp.bfloat16)
    query_grads = (mixed_grads.astype(jnp.float32) * convolved.astype(jnp.float32)).astype(jnp.bfloat16)
    conv_grads = (mixed_grads.astype(jnp.float32) * query_part.astype(jnp.float32)).astype(jnp.bfloat16)
    grad_blocks = conv_grads.astype(jnp.float32).reshape(GROUPS, GS, L // TAPS, TAPS)
    after_blocks = jnp.concatenate([grad_blocks[:, :, 1:], jnp.zeros_like(grad_blocks[:, :, :1])], axis=2)
    mixed_in_grads = jnp.einsum('gcnt,gbt->gcnb', grad_blocks, same_block, precision=HIGH) + jnp.einsum('gcnt,gbt->gcnb', after_blocks, prev_block, precision=HIGH)
    mixed_in_grads = mixed_in_grads.reshape(D, L).astype(jnp.bfloat16)
    within = jnp.einsum('gcns,gcnt->gst', blocks, grad_blocks, precision=HIGH)
    across = jnp.einsum('gcns,gcnt->gst', before, grad_blocks, precision=HIGH)
    filter_grads = jnp.einsum('gst,kst->gk', within, same_sel, precision=HIGH) + jnp.einsum('gst,kst->gk', across, prev_sel, precision=HIGH)
    key_grads = (mixed_in_grads.astype(jnp.float32) * value_part.astype(jnp.float32)).astype(jnp.bfloat16)
    value_grads = (mixed_in_grads.astype(jnp.float32) * key_part.astype(jnp.float32)).astype(jnp.bfloat16)
    proj_grads = jnp.stack([query_grads, key_grads, value_grads])
    in_weight_grads = ctx_partials(proj_grads, normed)
    norm_grads = jnp.einsum('poi,pot->it', in_weight.astype(jnp.float32), proj_grads.astype(jnp.float32), precision=HIGH)
    moment = lax.optimization_barrier(jnp.sum(norm_gain[:, None] * hidden_f * norm_grads, axis=0)) / D
    hidden_grads = out_grads.astype(jnp.float32) + rms_scale[None, :] * (norm_gain[:, None] * norm_grads - hidden_f * (rms_scale * rms_scale * moment)[None, :])
    return (layer_out, hidden_grads.astype(jnp.bfloat16), in_weight_grads, filter_grads, out_weight_grads)
```

```python
import functools

import jax
import jax.numpy as jnp
from jax import lax
from jax.experimental import pallas as pl
from jax.experimental.pallas import tpu as pltpu
from jax.sharding import Mesh, PartitionSpec as P

GS = 16
EPS = 1e-06
F32 = jnp.float32
BF = jnp.bfloat16
VM = pl.BlockSpec(memory_space=pltpu.VMEM)
SM = pl.BlockSpec(memory_space=pltpu.SMEM)
SWAP = [(0, 1), (1, 0)]


def shape(*dims, dtype=BF):
    return jax.ShapeDtypeStruct(dims, dtype)


def call(body, outs, *args, scratch=(), flops=0, moved=0, smem=True, name=None):
    specs = [SM if smem and i == 0 else VM for i in range(len(args))]
    multi = isinstance(outs, (list, tuple))
    return pl.pallas_call(
        body,
        out_shape=list(outs) if multi else outs,
        in_specs=specs,
        out_specs=[VM] * len(outs) if multi else VM,
        scratch_shapes=list(scratch),
        compiler_params=pltpu.CompilerParams(vmem_limit_bytes=28 * 2**20),
        cost_estimate=pl.CostEstimate(flops=flops, bytes_accessed=moved, transcendentals=0),
        name=name,
    )(*args)


def ring(size, step):
    return [(i, (i + step) % size) for i in range(size)]


def dot_nt(a, b):
    return lax.dot_general(a, b, (((1,), (1,)), ((), ())), preferred_element_type=F32)


def dot_tn(a, b):
    return lax.dot_general(a, b, (((0,), (0,)), ((), ())), preferred_element_type=F32)


def up(x):
    return x.astype(F32)


def toeplitz_body(filt_ref, fwd_ref, back_ref):
    n = filt_ref.shape[1]
    row = lax.broadcasted_iota(jnp.int32, (n, n), 0)
    col = lax.broadcasted_iota(jnp.int32, (n, n), 1)

    def group(g, _):
        mat = jnp.broadcast_to(filt_ref[pl.ds(g, 1), :], (n, n))
        step = 1
        while step < n:
            mat = jnp.where((row & step) != 0, pltpu.roll(mat, step, 1), mat)
            step *= 2
        same = jnp.where(col >= row, mat, 0.0).astype(BF)
        prev = jnp.where(col < row, mat, 0.0).astype(BF)
        fwd_ref[g, :n, :] = prev
        fwd_ref[g, n:, :] = same
        back_ref[g, :, :n] = same
        back_ref[g, :, n:] = prev
        return 0

    lax.fori_loop(0, filt_ref.shape[0], group, 0)


def piece_slots(ids):
    zh, y, c = ids[0], ids[1], ids[2]
    return [
        [z * 8 + lax.rem(y + 4 - s, 4) * 2 + k for s in range(4)]
        for z, k in ((zh, c), (1 - zh, c), (zh, 1 - c), (1 - zh, 1 - c))
    ]


def send_rows(ids, full_ref, own_ref, send_ref):
    c, x = ids[2], ids[3]
    for z in range(4):
        own_ref[z] = full_ref[z * 4 + x]
    for s in range(1, 4):
        dest = lax.rem(x + s, 4)
        for k in range(2):
            send_ref[s - 1, k] = full_ref[(2 * c + k) * 4 + dest]


def project_body(
    ids, gain_ref, w_ref, a_ref, b_ref, c_ref, d_ref,
    proj_ref, mixed_in_ref, tail_ref, rms_ref, own_ref, send_ref, full_ref,
):
    parts = (a_ref, b_ref, c_ref, d_ref)
    total = jnp.zeros((1, 256), F32)
    for part in parts:
        for s in range(4):
            h = up(part[s])
            total = total + jnp.sum(h * h, axis=0, keepdims=True)
    rms = lax.rsqrt(total * (1.0 / 4096.0) + EPS)
    rms_ref[...] = rms
    for part, slots in zip(parts, piece_slots(ids)):
        for s in range(4):
            gain = gain_ref[slots[s]]
            full_ref[slots[s]] = (up(part[s]) * rms * gain).astype(BF)

    normed = full_ref[...].reshape(4096, 256)
    for p in range(3):
        proj_ref[p] = jnp.dot(w_ref[p], normed, preferred_element_type=F32).astype(BF)
    mixed = (up(proj_ref[1]) * up(proj_ref[2])).astype(BF)
    mixed_in_ref[...] = mixed
    tail_ref[...] = mixed[:, 128:]
    send_rows(ids, full_ref, own_ref, send_ref)


def conv_body(x_ref, halo_ref, fwd_ref, proj_ref, conv_ref, mixed_ref):
    def group(g, _):
        rows = pl.ds(pl.multiple_of(g * GS, GS), GS)
        first = jnp.concatenate([halo_ref[rows, :], x_ref[rows, :128]], axis=1)
        both = jnp.concatenate([first, x_ref[rows, :]], axis=0)
        out = jnp.dot(both, fwd_ref[g], preferred_element_type=F32).astype(BF)
        conv = jnp.concatenate([out[:GS], out[GS:]], axis=1)
        conv_ref[rows, :] = conv
        mixed_ref[rows, :] = (up(proj_ref[0, rows, :]) * up(conv)).astype(BF)
        return 0

    lax.fori_loop(0, 16, group, 0, unroll=4)


def conv_back_body(
    g_ref, halo_ref, back_ref, proj_ref, qg_ref, kv_ref, part_ref, mig_ref
):
    def group(g, _):
        rows = pl.ds(pl.multiple_of(g * GS, GS), GS)
        second = jnp.concatenate([g_ref[rows, 128:], halo_ref[rows, :]], axis=1)
        both = jnp.concatenate([g_ref[rows, :], second], axis=0)
        out = dot_nt(both, back_ref[g]).astype(BF)
        mig_ref[rows, :] = jnp.concatenate([out[:GS], out[GS:]], axis=1)
        return 0

    lax.fori_loop(0, 16, group, 0, unroll=4)
    mig = up(mig_ref[...])
    key, value = up(proj_ref[1]), up(proj_ref[2])
    kg = (mig * value).astype(BF)
    vg = (mig * key).astype(BF)
    kv_ref[0] = kg
    kv_ref[1] = vg
    terms = up(qg_ref[...]) * up(proj_ref[0]) + up(kg) * key + up(vg) * value
    part_ref[...] = jnp.sum(terms, axis=0, keepdims=True)


def filter_grad_body(x_ref, halo_ref, g_ref, out_ref):
    n = 128
    row = lax.broadcasted_iota(jnp.int32, (n, n), 0)
    col = lax.broadcasted_iota(jnp.int32, (n, n), 1)

    def group(g, _):
        rows = pl.ds(pl.multiple_of(g * GS, GS), GS)
        first, second = x_ref[rows, :n], x_ref[rows, n:]
        grads = jnp.concatenate([g_ref[rows, :n], g_ref[rows, n:]], axis=0)
        here = jnp.concatenate([first, second], axis=0)
        before = jnp.concatenate([halo_ref[rows, :], first], axis=0)
        mat = jnp.where(col >= row, dot_tn(here, grads), dot_tn(before, grads))
        step = 1
        while step < n:
            mat = jnp.where((row & step) != 0, pltpu.roll(mat, n - step, 1), mat)
            step *= 2
        out_ref[pl.ds(g, 1), :] = jnp.sum(mat, axis=0, keepdims=True)
        return 0

    lax.fori_loop(0, 16, group, 0)


def rs_first_body(ids, w_ref, g_ref, out_ref):
    zh, y, c = ids[0], ids[1], ids[2]
    grads = [g_ref[p].T for p in range(g_ref.shape[0])]
    for zr, z in enumerate((zh, 1 - zh)):
        for s in range(4):
            slot = z * 8 + lax.rem(y + s, 4) * 2 + (1 - c)
            cols = pl.ds(pl.multiple_of(slot * 256, 256), 256)
            acc = jnp.dot(grads[0], w_ref[0, :, cols], preferred_element_type=F32)
            for p in range(1, len(grads)):
                acc += jnp.dot(grads[p], w_ref[p, :, cols], preferred_element_type=F32)
            out_ref[zr, s] = acc.astype(BF)


def rs_second_body(ids, w_ref, g_ref, recv_ref, *out_refs):
    zh, y, c = ids[0], ids[1], ids[2]
    grads = [g_ref[p].T for p in range(g_ref.shape[0])]
    for zr, z in ((1, 1 - zh), (0, zh)):
        for s in range(4):
            slot = z * 8 + lax.rem(y + s, 4) * 2 + c
            cols = pl.ds(pl.multiple_of(slot * 256, 256), 256)
            acc = up(recv_ref[zr, s])
            for p in range(len(grads)):
                acc += jnp.dot(grads[p], w_ref[p, :, cols], preferred_element_type=F32)
            out_refs[zr * 4 + s][...] = acc.astype(BF)


def reduce_scatter_tp(ids, weight, grads, name):
    planes = grads.shape[0]
    cost = 2 * 2048 * 256 * 256 * planes
    first = call(
        rs_first_body, shape(2, 4, 256, 256), ids, weight, grads,
        flops=cost, moved=planes * 2**20, name=name + "_a",
    )
    recv = lax.ppermute(first, "core", SWAP)
    blocks = call(
        rs_second_body, [shape(256, 256)] * 8, ids, weight, grads, recv,
        flops=cost, moved=planes * 2**20, name=name + "_b",
    )
    far = [blocks[4]] + [lax.ppermute(blocks[4 + s], "y", ring(4, s)) for s in (1, 2, 3)]
    far_sum = (up(far[0]) + up(far[1]) + up(far[2]) + up(far[3])).astype(BF)
    crossed = lax.ppermute(far_sum, "zh", SWAP)
    near = [blocks[0]] + [lax.ppermute(blocks[s], "y", ring(4, s)) for s in (1, 2, 3)]
    return near + [crossed]


def gather_tp(block):
    near = [block] + [lax.ppermute(block, "y", ring(4, s)) for s in (1, 2, 3)]
    other = lax.ppermute(block, "zh", SWAP)
    far = [other] + [lax.ppermute(other, "y", ring(4, s)) for s in (1, 2, 3)]
    near = jnp.stack(near)
    far = jnp.stack(far)
    return near, far, lax.ppermute(near, "core", SWAP), lax.ppermute(far, "core", SWAP)


def summed(refs):
    total = up(refs[0][...])
    for ref in refs[1:]:
        total = total + up(ref[...])
    return total


def mixed_grad_body(n0, n1, n2, n3, cr, conv_ref, proj_ref, qg_ref, cg_ref, head_ref):
    grads = up(summed((n0, n1, n2, n3, cr)).T.astype(BF))
    qg_ref[...] = (grads * up(conv_ref[...])).astype(BF)
    cg = (grads * up(proj_ref[0])).astype(BF)
    cg_ref[...] = cg
    head_ref[...] = cg[:, :128]


def hidden_grad_body(n0, n1, n2, n3, cr, hid_ref, og_ref, gain_ref, rms_ref, mom_ref, out_ref):
    grads = summed((n0, n1, n2, n3, cr)).T
    rms = rms_ref[...]
    moment = mom_ref[...] / (rms * 4096.0)
    out = up(og_ref[...]) + rms * (
        gain_ref[...] * grads - up(hid_ref[...]) * (rms * rms * moment)
    )
    out_ref[...] = out.astype(BF)


def out_body(ids, w_ref, hid_ref, a_ref, b_ref, c_ref, d_ref, out_ref, own_ref, send_ref, full_ref):
    for part, slots in zip((a_ref, b_ref, c_ref, d_ref), piece_slots(ids)):
        for s in range(4):
            full_ref[slots[s]] = part[s]
    mixed = full_ref[...].reshape(4096, 256)
    acc = jnp.dot(w_ref[...], mixed, preferred_element_type=F32)
    out_ref[...] = (up(hid_ref[...]) + acc).astype(BF)
    send_rows(ids, full_ref, own_ref, send_ref)


def weight_grad_body(ids, own_ref, n1, n2, n3, sw_ref, g0, g1, g2, g3, out_ref):
    c = ids[2]
    planes = g0.shape[0]
    recv = (n1, n2, n3)
    for half in range(2):
        for k in range(2):
            z = 2 * c + k if half == 0 else 2 * (1 - c) + k
            for p in range(planes):
                acc = dot_nt(g0[p], own_ref[z])
                for s, g in ((1, g1), (2, g2), (3, g3)):
                    rhs = recv[s - 1][k] if half == 0 else sw_ref[s - 1, k]
                    acc += dot_nt(g[p], rhs)
                out_ref[z, p] = acc.astype(BF)


def spread_x(own, send):
    recv = [lax.ppermute(send[s - 1], "x", ring(4, s)) for s in (1, 2, 3)]
    swapped = lax.ppermute(jnp.stack(recv), "core", SWAP)
    return own, *recv, swapped


def gather_x(block):
    return [block] + [lax.ppermute(block, "x", ring(4, s)) for s in (1, 2, 3)]


def weight_grads(ids, spread, grads, name):
    planes = grads[0].shape[0]
    part = call(
        weight_grad_body, shape(4, planes, 256, 256), ids, *spread, *grads,
        flops=2 * 1024 * 1024 * 256 * planes, moved=planes * 2**20, name=name,
    )
    return lax.psum_scatter(part, "zl", scatter_dimension=0, tiled=False).astype(F32)


def per_device(hidden_in, norm_gain, in_weight, filters, out_weight, out_grads):
    zl, x, zh, y, c = (lax.axis_index(name) for name in ("zl", "x", "zh", "y", "core"))
    ids = jnp.stack([zh, y, c, x, zl]).astype(jnp.int32)
    gain = norm_gain.reshape(16, 256, 1)
    tp = zh * 8 + y * 2 + c
    gain_rows = lax.dynamic_index_in_dim(gain, tp, 0, False)

    gathered = gather_tp(hidden_in)
    og = out_grads[None]
    mg_parts = reduce_scatter_tp(ids, out_weight[None], og, "mixed_grads")
    og_x = gather_x(og)
    fwd, back = call(
        toeplitz_body, [shape(16, 256, 128), shape(16, 128, 256)], filters, smem=False, name="taps"
    )

    proj, mixed_in, tail, rms, own, send = call(
        project_body,
        [
            shape(3, 256, 256), shape(256, 256), shape(256, 128), shape(1, 256, dtype=F32),
            shape(4, 256, 256), shape(3, 2, 256, 256),
        ],
        ids, gain, in_weight, *gathered,
        scratch=[pltpu.VMEM((16, 256, 256), BF)],
        flops=2 * 768 * 4096 * 256, moved=10 * 2**20, name="project",
    )
    halo = lax.ppermute(tail, ("zl", "x"), [(i, i + 1) for i in range(15)])
    conv, mixed = call(
        conv_body, [shape(256, 256)] * 2, mixed_in, halo, fwd, proj, smem=False,
        flops=2 * 256 * 256 * 256, name="conv",
    )
    qg, cg, head = call(
        mixed_grad_body, [shape(256, 256)] * 2 + [shape(256, 128)], *mg_parts, conv, proj,
        smem=False, name="mixed_grad",
    )
    next_halo = lax.ppermute(head, ("zl", "x"), [(i + 1, i) for i in range(15)])
    mixed_pieces = gather_tp(mixed)
    normed_x = spread_x(own, send)

    kv, part = call(
        conv_back_body, [shape(2, 256, 256), shape(1, 256, dtype=F32)],
        cg, next_halo, back, proj, qg, smem=False,
        scratch=[pltpu.VMEM((256, 256), BF)], flops=2 * 256 * 256 * 256, name="conv_back",
    )
    q_x = gather_x(qg[None])
    kv_x = gather_x(kv)
    in_q = weight_grads(ids, normed_x, q_x, "in_q")
    in_kv = weight_grads(ids, normed_x, kv_x, "in_kv")

    proj_grads = jnp.concatenate([qg[None], kv], axis=0)
    ng_parts = reduce_scatter_tp(ids, in_weight, proj_grads, "norm_grads")

    part = part + lax.ppermute(part, "core", SWAP)
    part = part + sum(lax.ppermute(part, "y", ring(4, s)) for s in (1, 2, 3))
    moment = part + lax.ppermute(part, "zh", SWAP)

    hidden_grads = call(
        hidden_grad_body, shape(256, 256), *ng_parts, hidden_in, out_grads, gain_rows, rms, moment,
        smem=False, name="hidden_grads",
    )

    layer_out, m_own, m_send = call(
        out_body, [shape(256, 256), shape(4, 256, 256), shape(3, 2, 256, 256)],
        ids, out_weight, hidden_in, *mixed_pieces,
        scratch=[pltpu.VMEM((16, 256, 256), BF)],
        flops=2 * 256 * 4096 * 256, moved=4 * 2**20, name="layer_out",
    )
    mixed_x = spread_x(m_own, m_send)
    out_w = weight_grads(ids, mixed_x, og_x, "out_w")

    taps = call(
        filter_grad_body, shape(16, 128, dtype=F32), mixed_in, halo, cg, smem=False,
        flops=2 * 256 * 256 * 256, name="tap_grads",
    )
    taps = taps.reshape(4, 4, 128)
    pick = lambda s: lax.dynamic_index_in_dim(taps, lax.rem(x + s, 4), 1, False)
    taps = pick(0) + sum(lax.ppermute(pick(s), "x", ring(4, s)) for s in (1, 2, 3))
    row = lambda s: lax.dynamic_index_in_dim(taps, lax.rem(zl + s, 4), 0, True)
    filter_grads = row(0) + sum(lax.ppermute(row(s), "zl", ring(4, s)) for s in (1, 2, 3))

    in_weight_grads = jnp.concatenate([in_q, in_kv], axis=0)
    return layer_out, hidden_grads, in_weight_grads, filter_grads, out_w[0]


def solution(mesh):
    fine = Mesh(mesh.devices.reshape(4, 4, 2, 4, 2), ("zl", "x", "zh", "y", "core"))
    tp, ctx = ("zh", "y", "core"), ("zl", "x")
    return jax.shard_map(
        per_device,
        mesh=fine,
        in_specs=(P(tp, ctx), P(), P(None, tp, None), P(tp, None), P(tp, None), P(tp, ctx)),
        out_specs=(P(tp, ctx), P(tp, ctx), P(None, tp, ctx), P(tp + ctx, None), P(tp, ctx)),
        check_vma=False,
    )
```

```python
import functools

import jax
import jax.numpy as jnp
from jax import lax
from jax.experimental import pallas as pl
from jax.experimental.pallas import tpu as pltpu
from jax.sharding import Mesh, PartitionSpec as P

GS = 16
EPS = 1e-06
F32 = jnp.float32
BF = jnp.bfloat16
VM = pl.BlockSpec(memory_space=pltpu.VMEM)
SM = pl.BlockSpec(memory_space=pltpu.SMEM)
HB = pl.BlockSpec(memory_space=pltpu.HBM)
SWAP = [(0, 1), (1, 0)]


def shape(*dims, dtype=BF):
    return jax.ShapeDtypeStruct(dims, dtype)


def call(body, outs, *args, scratch=(), flops=0, moved=0, smem=True, name=None, limit=14, hbm=()):
    specs = [SM if smem and i == 0 else HB if i in hbm else VM for i in range(len(args))]
    multi = isinstance(outs, (list, tuple))
    return pl.pallas_call(
        body,
        out_shape=list(outs) if multi else outs,
        in_specs=specs,
        out_specs=[VM] * len(outs) if multi else VM,
        scratch_shapes=list(scratch),
        compiler_params=pltpu.CompilerParams(vmem_limit_bytes=limit * 2**20),
        cost_estimate=pl.CostEstimate(flops=flops, bytes_accessed=moved, transcendentals=0),
        name=name,
    )(*args)


def ring(size, step):
    return [(i, (i + step) % size) for i in range(size)]


def after(value, *earlier):
    return lax.optimization_barrier((value, *earlier))[0]


def dot_nt(a, b):
    return lax.dot_general(a, b, (((1,), (1,)), ((), ())), preferred_element_type=F32)


def dot_tn(a, b):
    return lax.dot_general(a, b, (((0,), (0,)), ((), ())), preferred_element_type=F32)


def up(x):
    return x.astype(F32)


def toeplitz_body(filt_ref, fwd_ref, back_ref):
    n = filt_ref.shape[1]
    row = lax.broadcasted_iota(jnp.int32, (n, n), 0)
    col = lax.broadcasted_iota(jnp.int32, (n, n), 1)

    def group(g, _):
        mat = jnp.broadcast_to(filt_ref[pl.ds(g, 1), :], (n, n))
        step = 1
        while step < n:
            mat = jnp.where((row & step) != 0, pltpu.roll(mat, step, 1), mat)
            step *= 2
        same = jnp.where(col >= row, mat, 0.0).astype(BF)
        prev = jnp.where(col < row, mat, 0.0).astype(BF)
        fwd_ref[g, :n, :] = prev
        fwd_ref[g, n:, :] = same
        back_ref[g, :, :n] = same
        back_ref[g, :, n:] = prev
        return 0

    lax.fori_loop(0, filt_ref.shape[0], group, 0, unroll=8)


def piece_slots(ids):
    zh, y, c = ids[0], ids[1], ids[2]
    return [
        [z * 8 + lax.rem(y + 4 - s, 4) * 2 + k for s in range(4)]
        for z, k in ((zh, c), (1 - zh, c), (zh, 1 - c), (1 - zh, 1 - c))
    ]


def send_rows(ids, full_ref, send_refs):
    c, x = ids[2], ids[3]
    for s, send_ref in enumerate(send_refs):
        for k in range(2):
            send_ref[k] = full_ref[(2 * c + k) * 4 + lax.rem(x + s, 4)]


def project_body(
    ids, gain_ref, w_ref, a_ref, b_ref, c_ref, d_ref,
    proj_ref, mixed_in_ref, tail_ref, rms_ref, s0, s1, s2, s3, full_ref, w_buf, sems,
):
    copies = [pltpu.make_async_copy(w_ref.at[p], w_buf.at[p], sems.at[p]) for p in range(3)]
    for copy in copies:
        copy.start()
    parts = (a_ref, b_ref, c_ref, d_ref)
    total = jnp.zeros((1, 256), F32)
    for part in parts:
        for s in range(4):
            h = up(part[s])
            total = total + jnp.sum(h * h, axis=0, keepdims=True)
    rms = lax.rsqrt(total * (1.0 / 4096.0) + EPS)
    rms_ref[...] = rms
    gains = jnp.concatenate([gain_ref[...], jnp.zeros((112, 256), F32)], axis=0).T
    lane = lax.broadcasted_iota(jnp.int32, (256, 128), 1)
    for part, slots in zip(parts, piece_slots(ids)):
        for s in range(4):
            gain = jnp.sum(jnp.where(lane == slots[s], gains, 0.0), axis=1, keepdims=True)
            full_ref[slots[s]] = (up(part[s]) * rms * gain).astype(BF)

    normed = full_ref[...].reshape(4096, 256)
    for p in range(3):
        copies[p].wait()
        proj_ref[p] = jnp.dot(w_buf[p], normed, preferred_element_type=F32).astype(BF)
    mixed = (up(proj_ref[1]) * up(proj_ref[2])).astype(BF)
    mixed_in_ref[...] = mixed
    tail_ref[...] = mixed[:, 128:]
    send_rows(ids, full_ref, (s0, s1, s2, s3))


def conv_body(x_ref, halo_ref, fwd_ref, proj_ref, conv_ref, mixed_ref):
    def group(g, _):
        rows = pl.ds(pl.multiple_of(g * GS, GS), GS)
        first = jnp.concatenate([halo_ref[rows, :], x_ref[rows, :128]], axis=1)
        both = jnp.concatenate([first, x_ref[rows, :]], axis=0)
        out = jnp.dot(both, fwd_ref[g], preferred_element_type=F32).astype(BF)
        conv = jnp.concatenate([out[:GS], out[GS:]], axis=1)
        conv_ref[rows, :] = conv
        mixed_ref[rows, :] = (up(proj_ref[0, rows, :]) * up(conv)).astype(BF)
        return 0

    lax.fori_loop(0, 16, group, 0, unroll=4)


def conv_back_body(
    g_ref, halo_ref, back_ref, proj_ref, conv_ref, mg_ref, pg_ref, all_ref, part_ref, mig_ref
):
    def group(g, _):
        rows = pl.ds(pl.multiple_of(g * GS, GS), GS)
        second = jnp.concatenate([g_ref[rows, 128:], halo_ref[rows, :]], axis=1)
        both = jnp.concatenate([g_ref[rows, :], second], axis=0)
        out = dot_nt(both, back_ref[g]).astype(BF)
        mig_ref[rows, :] = jnp.concatenate([out[:GS], out[GS:]], axis=1)
        return 0

    lax.fori_loop(0, 16, group, 0, unroll=4)
    mig = up(mig_ref[...])
    key, value = up(proj_ref[1]), up(proj_ref[2])
    qg = (up(mg_ref[...]) * up(conv_ref[...])).astype(BF)
    kg = (mig * value).astype(BF)
    vg = (mig * key).astype(BF)
    pg_ref[0] = qg
    pg_ref[1] = kg
    pg_ref[2] = vg
    for dest in range(4):
        all_ref[dest] = pg_ref[...]
    terms = up(qg) * up(proj_ref[0]) + up(kg) * key + up(vg) * value
    part_ref[...] = jnp.sum(terms, axis=0, keepdims=True)


def filter_grad_body(x_ref, halo_ref, g_ref, out_ref):
    n = 128
    row = lax.broadcasted_iota(jnp.int32, (n, n), 0)
    col = lax.broadcasted_iota(jnp.int32, (n, n), 1)

    def group(g, _):
        rows = pl.ds(pl.multiple_of(g * GS, GS), GS)
        first, second = x_ref[rows, :n], x_ref[rows, n:]
        grads = jnp.concatenate([g_ref[rows, :n], g_ref[rows, n:]], axis=0)
        here = jnp.concatenate([first, second], axis=0)
        before = jnp.concatenate([halo_ref[rows, :], first], axis=0)
        mat = jnp.where(col >= row, dot_tn(here, grads), dot_tn(before, grads))
        step = 1
        while step < n:
            mat = jnp.where((row & step) != 0, pltpu.roll(mat, n - step, 1), mat)
            step *= 2
        out_ref[pl.ds(g, 1), :] = jnp.sum(mat, axis=0, keepdims=True)
        return 0

    lax.fori_loop(0, 16, group, 0, unroll=8)


def rs_first_body(ids, w_ref, g_ref, out_ref):
    zh, y, c = ids[0], ids[1], ids[2]
    grads = [g_ref[p].T for p in range(g_ref.shape[0])]
    for zr, z in enumerate((zh, 1 - zh)):
        for s in range(4):
            slot = z * 8 + lax.rem(y + s, 4) * 2 + (1 - c)
            cols = pl.ds(pl.multiple_of(slot * 256, 256), 256)
            acc = jnp.dot(grads[0], w_ref[0, :, cols], preferred_element_type=F32)
            for p in range(1, len(grads)):
                acc += jnp.dot(grads[p], w_ref[p, :, cols], preferred_element_type=F32)
            out_ref[zr, s] = acc.astype(BF)


def rs_second_body(riders, ids, w_ref, g_ref, recv_ref, *refs):
    rider_refs, out_refs = refs[:riders], refs[riders:]
    zh, y, c = ids[0], ids[1], ids[2]
    grads = [g_ref[p].T for p in range(g_ref.shape[0])]
    for s in (1, 3, 2, 0):
        for zr, z in ((1, 1 - zh), (0, zh)):
            slot = z * 8 + lax.rem(y + s, 4) * 2 + c
            cols = pl.ds(pl.multiple_of(slot * 256, 256), 256)
            acc = up(recv_ref[zr, s])
            for p in range(len(grads)):
                acc += jnp.dot(grads[p], w_ref[p, :, cols], preferred_element_type=F32)
            out_refs[s][zr] = acc.astype(BF)
        if s > 0:
            for rider in rider_refs:
                out_refs[s][2] = rider[...]


def combine_body(riders, *refs):
    parts, refs = refs[:4], refs[4:]
    own_riders, outs = refs[:riders], refs[riders:]
    for plane in range(2):
        total = up(parts[0][plane])
        for part in parts[1:]:
            total = total + up(part[plane])
        outs[plane][...] = total.astype(BF)
    for rider, out in zip(own_riders, outs[2:]):
        out[0] = rider[...]
        for s in (1, 2, 3):
            out[s] = parts[s][2]


def swap_products(ids, weight, grads, name):
    planes = grads.shape[0]
    first = call(
        rs_first_body, shape(2, 4, 256, 256), ids, weight, grads,
        flops=2 * 2048 * 256 * 256 * planes, moved=planes * 2**20, name=name + "_a",
    )
    return lax.ppermute(first, "core", SWAP)


def reduce_scatter_tp(ids, weight, grads, recv, name, *riders):
    planes = grads.shape[0]
    cost = 2 * 2048 * 256 * 256 * planes
    size = 2 + len(riders)
    blocks = call(
        functools.partial(rs_second_body, len(riders)),
        [shape(2, 256, 256)] + [shape(size, 256, 256)] * 3, ids, weight, grads, recv, *riders,
        flops=cost, moved=planes * 2**20, name=name + "_b",
    )
    parts = [blocks[0]] + [lax.ppermute(blocks[s], "y", ring(4, s)) for s in (1, 2, 3)]
    sums = call(
        functools.partial(combine_body, len(riders)),
        [shape(256, 256)] * 2 + [shape(4, 256, 256)] * len(riders), *parts, *riders,
        smem=False, name=name + "_sum",
    )
    return blocks[0], sums[0], lax.ppermute(sums[1], "zh", SWAP), *sums[2:]


def gather_tp(block, *earlier):
    near = [block] + [lax.ppermute(block, "y", ring(4, s)) for s in (1, 2, 3)]
    other = lax.ppermute(after(block, *earlier), "zh", SWAP)
    far = [other] + [lax.ppermute(other, "y", ring(4, s)) for s in (1, 2, 3)]
    near = jnp.stack(near)
    far = jnp.stack(far)
    return near, far, lax.ppermute(near, "core", SWAP), lax.ppermute(far, "core", SWAP)


def mixed_grad_body(near_ref, far_ref, proj_ref, mg_ref, cg_ref, head_ref):
    grads = (up(near_ref[...]) + up(far_ref[...])).T.astype(BF)
    mg_ref[...] = grads
    cg = (up(grads) * up(proj_ref[0])).astype(BF)
    cg_ref[...] = cg
    head_ref[...] = cg[:, :128]


def hidden_grad_body(near_ref, far_ref, hid_ref, og_ref, gain_ref, rms_ref, mom_ref, out_ref):
    grads = (up(near_ref[...]) + up(far_ref[...])).T
    rms = rms_ref[...]
    moment = mom_ref[...] / (rms * 4096.0)
    out = up(og_ref[...]) + rms * (
        gain_ref[...] * grads - up(hid_ref[...]) * (rms * rms * moment)
    )
    out_ref[...] = out.astype(BF)


def out_body(ids, w_ref, hid_ref, og_ref, a_ref, b_ref, c_ref, d_ref, out_ref, s0, s1, s2, s3, full_ref):
    for part, slots in zip((a_ref, b_ref, c_ref, d_ref), piece_slots(ids)):
        for s in range(4):
            full_ref[slots[s]] = part[s]
    mixed = full_ref[...].reshape(4096, 256)
    acc = jnp.dot(w_ref[...], mixed, preferred_element_type=F32)
    out_ref[...] = (up(hid_ref[...]) + acc).astype(BF)
    send_rows(ids, full_ref, (s0, s1, s2, s3))
    for send_ref in (s0, s1, s2, s3):
        send_ref[2] = og_ref[...]


def weight_grad_body(first, ids, m0, m1, m2, m3, other_ref, *refs):
    c, x = ids[2], ids[3]
    g_refs, out_ref = refs[:-1], refs[-1]
    planes = out_ref.shape[1]
    mine = (m0, m1, m2, m3)
    for core in range(2):
        for k in range(2):
            acc = None
            for s in range(4):
                g_ref = g_refs[0].at[lax.rem(x + 4 - s, 4)] if len(g_refs) == 1 else g_refs[s]
                left = g_ref[first : first + planes].reshape(planes * 256, 256)
                term = dot_nt(left, mine[s][k] if core == 0 else other_ref[s, k])
                acc = term if acc is None else acc + term
            z = 2 * (c if core == 0 else 1 - c) + k
            out_ref[z] = acc.astype(BF).reshape(planes, 256, 256)


def spread_x(send, *meanwhile):
    recv = [send[0]] + [lax.ppermute(send[s], "x", ring(4, s)) for s in (1, 2, 3)]
    stacked = jnp.stack([after(recv[0], *meanwhile)] + recv[1:])
    return *recv, lax.ppermute(stacked, "core", SWAP)


def weight_grads(ids, spread, grads, first, planes, name):
    return call(
        functools.partial(weight_grad_body, first), shape(4, planes, 256, 256),
        ids, *spread, *grads,
        flops=2 * 1024 * 1024 * 256 * planes, moved=planes * 2**20, name=name,
    )


def per_device(hidden_in, norm_gain, in_weight, filters, out_weight, out_grads):
    zl, x, zh, y, c = (lax.axis_index(name) for name in ("zl", "x", "zh", "y", "core"))
    ids = jnp.stack([zh, y, c, x, zl]).astype(jnp.int32)
    gain = norm_gain.reshape(16, 256)
    tp = zh * 8 + y * 2 + c
    gain_rows = lax.dynamic_slice_in_dim(norm_gain, tp * 256, 256, 0).reshape(256, 1)

    near = jnp.stack([hidden_in] + [lax.ppermute(hidden_in, "y", ring(4, s)) for s in (1, 2, 3)])
    near_swap = lax.ppermute(near, "core", SWAP)
    other = lax.ppermute(hidden_in, "zh", SWAP)
    fwd, back = call(
        toeplitz_body, [shape(16, 256, 128), shape(16, 128, 256)], after(filters, near), smem=False, name="taps"
    )
    og = out_grads[None]
    swapped = swap_products(ids, out_weight[None], og, "mixed_grads")
    _, *mg_parts, far = reduce_scatter_tp(
        ids, out_weight[None], og, swapped, "mixed_grads", after(other, near)
    )
    gathered = near, far, near_swap, lax.ppermute(far, "core", SWAP)
    proj, mixed_in, tail, rms, *send = call(
        project_body,
        [
            shape(3, 256, 256), shape(256, 256), shape(256, 128), shape(1, 256, dtype=F32),
            *[shape(2, 256, 256)] * 4,
        ],
        after(ids, mg_parts[0]), gain, in_weight, *gathered,
        scratch=[
            pltpu.VMEM((16, 256, 256), BF), pltpu.VMEM((3, 256, 4096), BF),
            pltpu.SemaphoreType.DMA((3,)),
        ],
        hbm=(2,), limit=22, flops=2 * 768 * 4096 * 256, moved=10 * 2**20, name="project",
    )
    halo = lax.ppermute(tail, ("zl", "x"), [(i, i + 1) for i in range(15)])
    mg, cg, head = call(
        mixed_grad_body, [shape(256, 256)] * 2 + [shape(256, 128)], *mg_parts, proj,
        smem=False, name="mixed_grad",
    )
    next_halo = lax.ppermute(head, ("zl", "x"), [(i + 1, i) for i in range(15)])
    conv, mixed = call(
        conv_body, [shape(256, 256)] * 2, mixed_in, after(halo, mg_parts[1]), fwd, proj, smem=False,
        flops=2 * 256 * 256 * 256, name="conv",
    )
    mixed_pieces = gather_tp(mixed, head)
    pg, pg_all, part = call(
        conv_back_body,
        [shape(3, 256, 256), shape(4, 3, 256, 256), shape(1, 256, dtype=F32)],
        cg, next_halo, back, proj, conv, mg, smem=False,
        scratch=[pltpu.VMEM((256, 256), BF)], flops=2 * 256 * 256 * 256, name="conv_back",
    )
    send = [send[0]] + [after(block, halo, next_halo) for block in send[1:]]
    normed_x = spread_x(send, pg)
    pg_x = lax.all_to_all(pg_all, "x", 0, 0, tiled=True)
    swapped = swap_products(ids, in_weight, pg, "norm_grads")
    in_part = weight_grads(
        ids, normed_x, [after(pg_x, mixed_pieces[0], swapped)], 0, 3, "in_w"
    )
    ng_block, *ng_parts = reduce_scatter_tp(
        ids, in_weight, pg, after(swapped, in_part), "norm_grads"
    )
    in_weight_grads = lax.psum_scatter(in_part, "zl", scatter_dimension=0, tiled=False).astype(F32)

    layer_out, *m_send = call(
        out_body, [shape(256, 256)] + [shape(3, 256, 256)] * 4,
        ids, after(out_weight, in_part, ng_block), hidden_in, out_grads, *mixed_pieces,
        scratch=[pltpu.VMEM((16, 256, 256), BF)],
        flops=2 * 256 * 4096 * 256, moved=4 * 2**20, name="layer_out",
    )
    taps = call(
        filter_grad_body, shape(16, 128, dtype=F32), mixed_in, halo, after(cg, in_part),
        smem=False, flops=2 * 256 * 256 * 256, name="tap_grads",
    )
    part = after(part, in_part)
    part = part + lax.ppermute(part, "core", SWAP)
    part = part + sum(lax.ppermute(part, "y", ring(4, s)) for s in (1, 2, 3))
    moment = part + lax.ppermute(part, "zh", SWAP)
    taps = taps.reshape(4, 4, 128)
    pick = lambda s: lax.dynamic_index_in_dim(taps, lax.rem(x + s, 4), 1, False)
    taps = pick(0) + sum(lax.ppermute(pick(s), "x", ring(4, s)) for s in (1, 2, 3))
    mixed_x = spread_x(m_send, taps, moment, ng_parts[0])
    out_part = weight_grads(ids, mixed_x, mixed_x[:4], 2, 1, "out_w")
    out_recv = lax.all_to_all(out_part[:, 0], "zl", 0, 0, tiled=True)
    out_weight_grads = jnp.sum(up(out_recv), axis=0)

    hidden_grads = call(
        hidden_grad_body, shape(256, 256), *ng_parts, hidden_in, out_grads, gain_rows, rms, moment,
        smem=False, name="hidden_grads",
    )

    row = lambda s: lax.dynamic_index_in_dim(taps, lax.rem(zl + s, 4), 0, True)
    filter_grads = row(0) + sum(lax.ppermute(row(s), "zl", ring(4, s)) for s in (1, 2, 3))

    return layer_out, hidden_grads, in_weight_grads, filter_grads, out_weight_grads


def solution(mesh):
    fine = Mesh(mesh.devices.reshape(4, 4, 2, 4, 2), ("zl", "x", "zh", "y", "core"))
    tp, ctx = ("zh", "y", "core"), ("zl", "x")
    return jax.shard_map(
        per_device,
        mesh=fine,
        in_specs=(P(tp, ctx), P(), P(None, tp, None), P(tp, None), P(tp, None), P(tp, ctx)),
        out_specs=(P(tp, ctx), P(tp, ctx), P(None, tp, ctx), P(tp + ctx, None), P(tp, ctx)),
        check_vma=False,
    )
```

```python
import functools

import jax
import jax.numpy as jnp
from jax import lax
from jax.experimental import pallas as pl
from jax.experimental.pallas import tpu as pltpu
from jax.sharding import Mesh, PartitionSpec as P

GS = 16
EPS = 1e-06
F32 = jnp.float32
BF = jnp.bfloat16
VM = pl.BlockSpec(memory_space=pltpu.VMEM)
SM = pl.BlockSpec(memory_space=pltpu.SMEM)
SWAP = [(0, 1), (1, 0)]


def shape(*dims, dtype=BF):
    return jax.ShapeDtypeStruct(dims, dtype)


def call(body, outs, *args, scratch=(), flops=0, moved=0, smem=True, name=None, limit=10):
    specs = [SM if smem and i == 0 else VM for i in range(len(args))]
    multi = isinstance(outs, (list, tuple))
    return pl.pallas_call(
        body,
        out_shape=list(outs) if multi else outs,
        in_specs=specs,
        out_specs=[VM] * len(outs) if multi else VM,
        scratch_shapes=list(scratch),
        compiler_params=pltpu.CompilerParams(vmem_limit_bytes=limit * 2**20),
        cost_estimate=pl.CostEstimate(flops=flops, bytes_accessed=moved, transcendentals=0),
        name=name,
    )(*args)


def ring(size, step):
    return [(i, (i + step) % size) for i in range(size)]


def after(value, *earlier):
    return lax.optimization_barrier((value, *earlier))[0]


def dot_nt(a, b):
    return lax.dot_general(a, b, (((1,), (1,)), ((), ())), preferred_element_type=F32)


def dot_tn(a, b):
    return lax.dot_general(a, b, (((0,), (0,)), ((), ())), preferred_element_type=F32)


def up(x):
    return x.astype(F32)


def toeplitz_body(filt_ref, fwd_ref, back_ref):
    n = filt_ref.shape[1]
    row = lax.broadcasted_iota(jnp.int32, (n, n), 0)
    col = lax.broadcasted_iota(jnp.int32, (n, n), 1)

    def group(g, _):
        mat = jnp.broadcast_to(filt_ref[pl.ds(g, 1), :], (n, n))
        step = 1
        while step < n:
            mat = jnp.where((row & step) != 0, pltpu.roll(mat, step, 1), mat)
            step *= 2
        same = jnp.where(col >= row, mat, 0.0).astype(BF)
        prev = jnp.where(col < row, mat, 0.0).astype(BF)
        fwd_ref[g, :n, :] = prev
        fwd_ref[g, n:, :] = same
        back_ref[g, :, :n] = same
        back_ref[g, :, n:] = prev
        return 0

    lax.fori_loop(0, filt_ref.shape[0], group, 0, unroll=8)


def piece_slots(ids):
    zh, y, c = ids[0], ids[1], ids[2]
    return [
        [z * 8 + lax.rem(y + 4 - s, 4) * 2 + k for s in range(4)]
        for z, k in ((zh, c), (1 - zh, c), (zh, 1 - c), (1 - zh, 1 - c))
    ]


def send_rows(ids, full_ref, send_refs):
    c, x = ids[2], ids[3]
    for s, send_ref in enumerate(send_refs):
        for k in range(2):
            send_ref[k] = full_ref[(2 * c + k) * 4 + lax.rem(x + s, 4)]


def project_body(
    ids, gain_ref, w_ref, a_ref, b_ref, c_ref, d_ref,
    proj_ref, mixed_in_ref, tail_ref, rms_ref, s0, s1, s2, s3, full_ref,
):
    parts = (a_ref, b_ref, c_ref, d_ref)
    total = jnp.zeros((1, 256), F32)
    for part in parts:
        for s in range(4):
            h = up(part[s])
            total = total + jnp.sum(h * h, axis=0, keepdims=True)
    rms = lax.rsqrt(total * (1.0 / 4096.0) + EPS)
    rms_ref[...] = rms
    gains = jnp.concatenate([gain_ref[...], jnp.zeros((112, 256), F32)], axis=0).T
    lane = lax.broadcasted_iota(jnp.int32, (256, 128), 1)
    for part, slots in zip(parts, piece_slots(ids)):
        for s in range(4):
            gain = jnp.sum(jnp.where(lane == slots[s], gains, 0.0), axis=1, keepdims=True)
            full_ref[slots[s]] = (up(part[s]) * rms * gain).astype(BF)

    normed = full_ref[...].reshape(4096, 256)
    for p in range(3):
        proj_ref[p] = jnp.dot(w_ref[p], normed, preferred_element_type=F32).astype(BF)
    mixed = (up(proj_ref[1]) * up(proj_ref[2])).astype(BF)
    mixed_in_ref[...] = mixed
    tail_ref[...] = mixed[:, 128:]
    send_rows(ids, full_ref, (s0, s1, s2, s3))


def conv_body(x_ref, halo_ref, fwd_ref, proj_ref, conv_ref, mixed_ref):
    def group(g, _):
        rows = pl.ds(pl.multiple_of(g * GS, GS), GS)
        first = jnp.concatenate([halo_ref[rows, :], x_ref[rows, :128]], axis=1)
        both = jnp.concatenate([first, x_ref[rows, :]], axis=0)
        out = jnp.dot(both, fwd_ref[g], preferred_element_type=F32).astype(BF)
        conv = jnp.concatenate([out[:GS], out[GS:]], axis=1)
        conv_ref[rows, :] = conv
        mixed_ref[rows, :] = (up(proj_ref[0, rows, :]) * up(conv)).astype(BF)
        return 0

    lax.fori_loop(0, 16, group, 0, unroll=4)


def conv_back_body(
    g_ref, halo_ref, back_ref, proj_ref, conv_ref, mg_ref, pg_ref, all_ref, part_ref, mig_ref
):
    def group(g, _):
        rows = pl.ds(pl.multiple_of(g * GS, GS), GS)
        second = jnp.concatenate([g_ref[rows, 128:], halo_ref[rows, :]], axis=1)
        both = jnp.concatenate([g_ref[rows, :], second], axis=0)
        out = dot_nt(both, back_ref[g]).astype(BF)
        mig_ref[rows, :] = jnp.concatenate([out[:GS], out[GS:]], axis=1)
        return 0

    lax.fori_loop(0, 16, group, 0, unroll=4)
    mig = up(mig_ref[...])
    key, value = up(proj_ref[1]), up(proj_ref[2])
    qg = (up(mg_ref[...]) * up(conv_ref[...])).astype(BF)
    kg = (mig * value).astype(BF)
    vg = (mig * key).astype(BF)
    pg_ref[0] = qg
    pg_ref[1] = kg
    pg_ref[2] = vg
    for dest in range(4):
        all_ref[dest] = pg_ref[...]
    terms = up(qg) * up(proj_ref[0]) + up(kg) * key + up(vg) * value
    part_ref[...] = jnp.sum(terms, axis=0, keepdims=True)


def filter_grad_body(x_ref, halo_ref, g_ref, out_ref):
    n = 128
    row = lax.broadcasted_iota(jnp.int32, (n, n), 0)
    col = lax.broadcasted_iota(jnp.int32, (n, n), 1)

    def group(g, _):
        rows = pl.ds(pl.multiple_of(g * GS, GS), GS)
        first, second = x_ref[rows, :n], x_ref[rows, n:]
        grads = jnp.concatenate([g_ref[rows, :n], g_ref[rows, n:]], axis=0)
        here = jnp.concatenate([first, second], axis=0)
        before = jnp.concatenate([halo_ref[rows, :], first], axis=0)
        mat = jnp.where(col >= row, dot_tn(here, grads), dot_tn(before, grads))
        step = 1
        while step < n:
            mat = jnp.where((row & step) != 0, pltpu.roll(mat, n - step, 1), mat)
            step *= 2
        out_ref[pl.ds(g, 1), :] = jnp.sum(mat, axis=0, keepdims=True)
        return 0

    lax.fori_loop(0, 16, group, 0, unroll=8)


def rs_first_body(ids, w_ref, g_ref, out_ref):
    zh, y, c = ids[0], ids[1], ids[2]
    grads = [g_ref[p].T for p in range(g_ref.shape[0])]
    for zr, z in enumerate((zh, 1 - zh)):
        for s in range(4):
            slot = z * 8 + lax.rem(y + s, 4) * 2 + (1 - c)
            cols = pl.ds(pl.multiple_of(slot * 256, 256), 256)
            acc = jnp.dot(grads[0], w_ref[0, :, cols], preferred_element_type=F32)
            for p in range(1, len(grads)):
                acc += jnp.dot(grads[p], w_ref[p, :, cols], preferred_element_type=F32)
            out_ref[zr, s] = acc.astype(BF)


def split_sum(value):
    high = up(value.astype(BF))
    row = lax.broadcasted_iota(jnp.int32, (16, value.shape[1]), 0)
    return jnp.where(row == 0, high, jnp.where(row == 1, value - high, 0.0)).astype(BF)


def rs_second_body(ids, w_ref, g_ref, recv_ref, rider_ref, *out_refs):
    zh, y, c = ids[0], ids[1], ids[2]
    grads = [g_ref[p].T for p in range(g_ref.shape[0])]
    for s in (1, 3, 2, 0):
        for zr, z in ((1, 1 - zh), (0, zh)):
            slot = z * 8 + lax.rem(y + s, 4) * 2 + c
            cols = pl.ds(pl.multiple_of(slot * 256, 256), 256)
            acc = up(recv_ref[zr, s])
            for p in range(len(grads)):
                acc += jnp.dot(grads[p], w_ref[p, :, cols], preferred_element_type=F32)
            out_refs[s][zr * 256 : zr * 256 + 256, :] = acc.astype(BF)
        if rider_ref.shape[0] == 1:
            out_refs[s][512:, :] = split_sum(rider_ref[...])
        else:
            out_refs[s][512:, :] = rider_ref[...]


def combine_body(p0, p1, p2, p3, near_ref, far_ref, rider_ref):
    parts = (p0, p1, p2, p3)

    def total(rows):
        return up(p0[rows, :]) + up(p1[rows, :]) + up(p2[rows, :]) + up(p3[rows, :])

    near_ref[...] = total(slice(0, 256)).astype(BF)
    far_ref[:256, :] = total(slice(256, 512)).astype(BF)
    if rider_ref.shape[0] == 1:
        row = jnp.sum(total(slice(512, 528)), axis=0, keepdims=True)
        rider_ref[...] = row
        far_ref[256:, :] = split_sum(row)
    else:
        for s, part in enumerate(parts):
            rider_ref[s] = part[512:, :]


def swap_products(ids, weight, grads, name):
    planes = grads.shape[0]
    first = call(
        rs_first_body, shape(2, 4, 256, 256), ids, weight, grads,
        flops=2 * 2048 * 256 * 256 * planes, moved=planes * 2**20, name=name + "_a",
    )
    return lax.ppermute(first, "core", SWAP)


def reduce_scatter_tp(ids, weight, grads, recv, rider, name):
    planes = grads.shape[0]
    summed = rider.shape[0] == 1
    rows = 528 if summed else 768
    blocks = call(
        rs_second_body, [shape(rows, 256)] * 4, ids, weight, grads, recv, rider,
        flops=2 * 2048 * 256 * 256 * planes, moved=planes * 2**20, name=name + "_b",
    )
    parts = [blocks[0]] + [lax.ppermute(blocks[s], "y", ring(4, s)) for s in (1, 2, 3)]
    near, far, riders = call(
        combine_body,
        [
            shape(256, 256), shape(272 if summed else 256, 256),
            shape(1, 256, dtype=F32) if summed else shape(4, 256, 256),
        ],
        *parts, smem=False, name=name + "_sum",
    )
    return blocks[0], near, lax.ppermute(far, "zh", SWAP), riders


def gather_tp(block):
    near = [block] + [lax.ppermute(block, "y", ring(4, s)) for s in (1, 2, 3)]
    other = lax.ppermute(block, "zh", SWAP)
    far = [other] + [lax.ppermute(other, "y", ring(4, s)) for s in (1, 2, 3)]
    near = jnp.stack(near)
    far = jnp.stack(far)
    return near, far, lax.ppermute(near, "core", SWAP), lax.ppermute(far, "core", SWAP)


def mixed_grad_body(near_ref, far_ref, proj_ref, mg_ref, cg_ref, head_ref):
    grads = (up(near_ref[...]) + up(far_ref[...])).T.astype(BF)
    mg_ref[...] = grads
    cg = (up(grads) * up(proj_ref[0])).astype(BF)
    cg_ref[...] = cg
    head_ref[...] = cg[:, :128]


def hidden_grad_body(near_ref, far_ref, hid_ref, og_ref, gain_ref, rms_ref, mom_ref, out_ref):
    grads = (up(near_ref[...]) + up(far_ref[:256, :])).T
    rms = rms_ref[...]
    total = mom_ref[...] + jnp.sum(up(far_ref[256:, :]), axis=0, keepdims=True)
    moment = total / (rms * 4096.0)
    out = up(og_ref[...]) + rms * (
        gain_ref[...] * grads - up(hid_ref[...]) * (rms * rms * moment)
    )
    out_ref[...] = out.astype(BF)


def out_body(ids, w_ref, hid_ref, og_ref, a_ref, b_ref, c_ref, d_ref, out_ref, send_ref, full_ref):
    for part, slots in zip((a_ref, b_ref, c_ref, d_ref), piece_slots(ids)):
        for s in range(4):
            full_ref[slots[s]] = part[s]
    mixed = full_ref[...].reshape(4096, 256)
    acc = jnp.dot(w_ref[...], mixed, preferred_element_type=F32)
    out_ref[...] = (up(hid_ref[...]) + acc).astype(BF)
    for dest in range(4):
        for k in range(2):
            send_ref[dest, k] = full_ref[(2 * ids[2] + k) * 4 + dest]
        send_ref[dest, 2] = og_ref[...]


def weight_grad_body(relative, first, ids, mine_ref, other_ref, g_ref, out_ref):
    c, x = ids[2], ids[3]
    planes = out_ref.shape[1]
    for core, ref in ((c, mine_ref), (1 - c, other_ref)):
        for k in range(2):
            acc = None
            for s in range(4):
                at = lax.rem(x + 4 - s, 4) if relative else s
                left = g_ref[at, first : first + planes].reshape(planes * 256, 256)
                term = dot_nt(left, ref[s, k])
                acc = term if acc is None else acc + term
            out_ref[2 * core + k] = acc.astype(BF).reshape(planes, 256, 256)


def weight_grads(ids, mine, other, grads, relative, first, planes, name):
    return call(
        functools.partial(weight_grad_body, relative, first), shape(4, planes, 256, 256),
        ids, mine, other, grads,
        flops=2 * 1024 * 1024 * 256 * planes, moved=planes * 2**20, name=name,
    )


def per_device(hidden_in, norm_gain, in_weight, filters, out_weight, out_grads):
    zl, x, zh, y, c = (lax.axis_index(name) for name in ("zl", "x", "zh", "y", "core"))
    ids = jnp.stack([zh, y, c, x, zl]).astype(jnp.int32)
    gain = norm_gain.reshape(16, 256)
    tp = zh * 8 + y * 2 + c
    gain_rows = lax.dynamic_slice_in_dim(norm_gain, tp * 256, 256, 0).reshape(256, 1)

    near = jnp.stack([hidden_in] + [lax.ppermute(hidden_in, "y", ring(4, s)) for s in (1, 2, 3)])
    near_swap = lax.ppermute(near, "core", SWAP)
    other = lax.ppermute(hidden_in, "zh", SWAP)
    fwd, back = call(
        toeplitz_body, [shape(16, 256, 128), shape(16, 128, 256)], after(filters, near), smem=False, name="taps"
    )
    og = out_grads[None]
    swapped = swap_products(ids, out_weight[None], og, "mixed_grads")
    _, *mg_parts, far = reduce_scatter_tp(
        ids, out_weight[None], og, swapped, after(other, near), "mixed_grads"
    )
    gathered = near, far, near_swap, lax.ppermute(far, "core", SWAP)
    proj, mixed_in, tail, rms, *send = call(
        project_body,
        [
            shape(3, 256, 256), shape(256, 256), shape(256, 128), shape(1, 256, dtype=F32),
            *[shape(2, 256, 256)] * 4,
        ],
        after(ids, mg_parts[0]), gain, in_weight, *gathered,
        scratch=[pltpu.VMEM((16, 256, 256), BF)],
        flops=2 * 768 * 4096 * 256, moved=10 * 2**20, name="project",
    )
    halo = lax.ppermute(tail, ("zl", "x"), [(i, i + 1) for i in range(15)])
    mg, cg, head = call(
        mixed_grad_body, [shape(256, 256)] * 2 + [shape(256, 128)], *mg_parts, proj,
        smem=False, name="mixed_grad",
    )
    next_halo = lax.ppermute(head, ("zl", "x"), [(i + 1, i) for i in range(15)])
    conv, mixed = call(
        conv_body, [shape(256, 256)] * 2, mixed_in, after(halo, mg_parts[1]), fwd, proj, smem=False,
        flops=2 * 256 * 256 * 256, name="conv",
    )
    pg, pg_all, part = call(
        conv_back_body,
        [shape(3, 256, 256), shape(4, 3, 256, 256), shape(1, 256, dtype=F32)],
        cg, next_halo, back, proj, conv, mg, smem=False,
        scratch=[pltpu.VMEM((256, 256), BF)], flops=2 * 256 * 256 * 256, name="conv_back",
    )
    mixed_pieces = gather_tp(after(mixed, pg))
    send = [send[0]] + [after(block, pg) for block in send[1:]]
    normed_x = [send[0]] + [lax.ppermute(send[s], "x", ring(4, s)) for s in (1, 2, 3)]
    normed_x = jnp.stack([after(normed_x[0], pg, *mixed_pieces[:2])] + normed_x[1:])
    normed_other = lax.ppermute(normed_x, "core", SWAP)
    pg_x = lax.all_to_all(pg_all, "x", 0, 0, tiled=True)
    swapped = swap_products(ids, in_weight, after(pg, normed_x), "norm_grads")
    part = part + lax.ppermute(part, "core", SWAP)
    ng_block, *ng_parts = reduce_scatter_tp(
        ids, in_weight, pg, swapped, part, "norm_grads"
    )
    in_part = weight_grads(
        ids, normed_x, normed_other, after(pg_x, mixed_pieces[0], ng_block), True, 0, 3, "in_w"
    )
    in_weight_grads = lax.psum_scatter(in_part, "zl", scatter_dimension=0, tiled=False).astype(F32)

    layer_out, m_send = call(
        out_body, [shape(256, 256), shape(4, 3, 256, 256)],
        ids, after(out_weight, in_part), hidden_in, out_grads, *mixed_pieces,
        scratch=[pltpu.VMEM((16, 256, 256), BF)],
        flops=2 * 256 * 4096 * 256, moved=4 * 2**20, name="layer_out",
    )
    taps = call(
        filter_grad_body, shape(16, 128, dtype=F32), mixed_in, halo, after(cg, m_send),
        smem=False, flops=2 * 256 * 256 * 256, name="tap_grads",
    )
    taps = taps.reshape(4, 4, 128)
    pick = lambda s: lax.dynamic_index_in_dim(taps, lax.rem(x + s, 4), 1, False)
    taps = pick(0) + sum(lax.ppermute(pick(s), "x", ring(4, s)) for s in (1, 2, 3))
    mixed_x = lax.all_to_all(m_send, "x", 0, 0, tiled=True)
    mixed_other = lax.ppermute(after(mixed_x, taps, ng_parts[0]), "core", SWAP)
    out_part = weight_grads(ids, mixed_x, mixed_other, mixed_x, False, 2, 1, "out_w")
    out_recv = lax.all_to_all(out_part[:, 0], "zl", 0, 0, tiled=True)
    out_weight_grads = jnp.sum(up(out_recv), axis=0)

    hidden_grads = call(
        hidden_grad_body, shape(256, 256), *ng_parts[:2], hidden_in, out_grads, gain_rows, rms, ng_parts[2],
        smem=False, name="hidden_grads",
    )

    row = lambda s: lax.dynamic_index_in_dim(taps, lax.rem(zl + s, 4), 0, True)
    filter_grads = row(0) + sum(lax.ppermute(row(s), "zl", ring(4, s)) for s in (1, 2, 3))

    return layer_out, hidden_grads, in_weight_grads, filter_grads, out_weight_grads


def solution(mesh):
    fine = Mesh(mesh.devices.reshape(4, 4, 2, 4, 2), ("zl", "x", "zh", "y", "core"))
    tp, ctx = ("zh", "y", "core"), ("zl", "x")
    return jax.shard_map(
        per_device,
        mesh=fine,
        in_specs=(P(tp, ctx), P(), P(None, tp, None), P(tp, None), P(tp, None), P(tp, ctx)),
        out_specs=(P(tp, ctx), P(tp, ctx), P(None, tp, ctx), P(tp + ctx, None), P(tp, ctx)),
        check_vma=False,
    )
```

```python
import functools

import jax
import jax.numpy as jnp
from jax import lax
from jax.experimental import pallas as pl
from jax.experimental.pallas import tpu as pltpu
from jax.sharding import Mesh, PartitionSpec as P

GS = 16
EPS = 1e-06
F32 = jnp.float32
BF = jnp.bfloat16
VM = pl.BlockSpec(memory_space=pltpu.VMEM)
SM = pl.BlockSpec(memory_space=pltpu.SMEM)
SWAP = [(0, 1), (1, 0)]


def shape(*dims, dtype=BF):
    return jax.ShapeDtypeStruct(dims, dtype)


def call(body, outs, *args, scratch=(), flops=0, moved=0, smem=True, name=None, limit=10):
    specs = [SM if smem and i == 0 else VM for i in range(len(args))]
    multi = isinstance(outs, (list, tuple))
    return pl.pallas_call(
        body,
        out_shape=list(outs) if multi else outs,
        in_specs=specs,
        out_specs=[VM] * len(outs) if multi else VM,
        scratch_shapes=list(scratch),
        compiler_params=pltpu.CompilerParams(vmem_limit_bytes=limit * 2**20),
        cost_estimate=pl.CostEstimate(flops=flops, bytes_accessed=moved, transcendentals=0),
        name=name,
    )(*args)


def ring(size, step):
    return [(i, (i + step) % size) for i in range(size)]


def after(value, *earlier):
    return lax.optimization_barrier((value, *earlier))[0]


def dot_nt(a, b):
    return lax.dot_general(a, b, (((1,), (1,)), ((), ())), preferred_element_type=F32)


def dot_tn(a, b):
    return lax.dot_general(a, b, (((0,), (0,)), ((), ())), preferred_element_type=F32)


def up(x):
    return x.astype(F32)


def toeplitz_body(filt_ref, fwd_ref, back_ref):
    n = filt_ref.shape[1]
    row = lax.broadcasted_iota(jnp.int32, (n, n), 0)
    col = lax.broadcasted_iota(jnp.int32, (n, n), 1)

    def group(g, _):
        mat = jnp.broadcast_to(filt_ref[pl.ds(g, 1), :], (n, n))
        step = 1
        while step < n:
            mat = jnp.where((row & step) != 0, pltpu.roll(mat, step, 1), mat)
            step *= 2
        same = jnp.where(col >= row, mat, 0.0).astype(BF)
        prev = jnp.where(col < row, mat, 0.0).astype(BF)
        fwd_ref[g, :n, :] = prev
        fwd_ref[g, n:, :] = same
        back_ref[g, :, :n] = same
        back_ref[g, :, n:] = prev
        return 0

    lax.fori_loop(0, filt_ref.shape[0], group, 0, unroll=8)


def piece_slots(ids):
    zh, y, c = ids[0], ids[1], ids[2]
    return [
        [z * 8 + lax.rem(y + 4 - s, 4) * 2 + k for s in range(4)]
        for z, k in ((zh, c), (1 - zh, c), (zh, 1 - c), (1 - zh, 1 - c))
    ]


def send_rows(ids, full_ref, send_refs):
    c, x = ids[2], ids[3]
    for s, send_ref in enumerate(send_refs):
        for k in range(2):
            send_ref[k] = full_ref[(2 * c + k) * 4 + lax.rem(x + s, 4)]


def project_body(
    ids, gain_ref, w_ref, a_ref, b_ref, c_ref, d_ref,
    proj_ref, mixed_in_ref, tail_ref, rms_ref, s0, s1, s2, s3, full_ref,
):
    parts = (a_ref, b_ref, c_ref, d_ref)
    total = jnp.zeros((1, 256), F32)
    for part in parts:
        for s in range(4):
            h = up(part[s])
            total = total + jnp.sum(h * h, axis=0, keepdims=True)
    rms = lax.rsqrt(total * (1.0 / 4096.0) + EPS)
    rms_ref[...] = rms
    gains = jnp.concatenate([gain_ref[...], jnp.zeros((112, 256), F32)], axis=0).T
    lane = lax.broadcasted_iota(jnp.int32, (256, 128), 1)
    for part, slots in zip(parts, piece_slots(ids)):
        for s in range(4):
            gain = jnp.sum(jnp.where(lane == slots[s], gains, 0.0), axis=1, keepdims=True)
            full_ref[slots[s]] = (up(part[s]) * rms * gain).astype(BF)

    normed = full_ref[...].reshape(4096, 256)
    for p in range(3):
        proj_ref[p] = jnp.dot(w_ref[p], normed, preferred_element_type=F32).astype(BF)
    mixed = (up(proj_ref[1]) * up(proj_ref[2])).astype(BF)
    mixed_in_ref[...] = mixed
    tail_ref[...] = mixed[:, 128:]
    send_rows(ids, full_ref, (s0, s1, s2, s3))


def conv_body(x_ref, halo_ref, fwd_ref, proj_ref, conv_ref, mixed_ref):
    def group(g, _):
        rows = pl.ds(pl.multiple_of(g * GS, GS), GS)
        first = jnp.concatenate([halo_ref[rows, :], x_ref[rows, :128]], axis=1)
        both = jnp.concatenate([first, x_ref[rows, :]], axis=0)
        out = jnp.dot(both, fwd_ref[g], preferred_element_type=F32).astype(BF)
        conv = jnp.concatenate([out[:GS], out[GS:]], axis=1)
        conv_ref[rows, :] = conv
        mixed_ref[rows, :] = (up(proj_ref[0, rows, :]) * up(conv)).astype(BF)
        return 0

    lax.fori_loop(0, 16, group, 0, unroll=4)


def conv_back_body(
    g_ref, halo_ref, back_ref, proj_ref, conv_ref, mg_ref, pg_ref, all_ref, part_ref, mig_ref
):
    def group(g, _):
        rows = pl.ds(pl.multiple_of(g * GS, GS), GS)
        second = jnp.concatenate([g_ref[rows, 128:], halo_ref[rows, :]], axis=1)
        both = jnp.concatenate([g_ref[rows, :], second], axis=0)
        out = dot_nt(both, back_ref[g]).astype(BF)
        mig_ref[rows, :] = jnp.concatenate([out[:GS], out[GS:]], axis=1)
        return 0

    lax.fori_loop(0, 16, group, 0, unroll=4)
    mig = up(mig_ref[...])
    key, value = up(proj_ref[1]), up(proj_ref[2])
    qg = (up(mg_ref[...]) * up(conv_ref[...])).astype(BF)
    kg = (mig * value).astype(BF)
    vg = (mig * key).astype(BF)
    pg_ref[0] = qg
    pg_ref[1] = kg
    pg_ref[2] = vg
    for dest in range(4):
        all_ref[dest] = pg_ref[...]
    terms = up(qg) * up(proj_ref[0]) + up(kg) * key + up(vg) * value
    part_ref[...] = jnp.sum(terms, axis=0, keepdims=True)


def filter_grad_body(x_ref, halo_ref, g_ref, out_ref):
    n = 128
    row = lax.broadcasted_iota(jnp.int32, (n, n), 0)
    col = lax.broadcasted_iota(jnp.int32, (n, n), 1)

    def group(g, _):
        rows = pl.ds(pl.multiple_of(g * GS, GS), GS)
        first, second = x_ref[rows, :n], x_ref[rows, n:]
        grads = jnp.concatenate([g_ref[rows, :n], g_ref[rows, n:]], axis=0)
        here = jnp.concatenate([first, second], axis=0)
        before = jnp.concatenate([halo_ref[rows, :], first], axis=0)
        mat = jnp.where(col >= row, dot_tn(here, grads), dot_tn(before, grads))
        step = 1
        while step < n:
            mat = jnp.where((row & step) != 0, pltpu.roll(mat, n - step, 1), mat)
            step *= 2
        out_ref[pl.ds(g, 1), :] = jnp.sum(mat, axis=0, keepdims=True)
        return 0

    lax.fori_loop(0, 16, group, 0, unroll=8)


def rs_first_body(ids, w_ref, g_ref, out_ref):
    zh, y, c = ids[0], ids[1], ids[2]
    grads = [g_ref[p].T for p in range(g_ref.shape[0])]
    for zr, z in enumerate((zh, 1 - zh)):
        for s in range(4):
            slot = z * 8 + lax.rem(y + s, 4) * 2 + (1 - c)
            cols = pl.ds(pl.multiple_of(slot * 256, 256), 256)
            acc = jnp.dot(grads[0], w_ref[0, :, cols], preferred_element_type=F32)
            for p in range(1, len(grads)):
                acc += jnp.dot(grads[p], w_ref[p, :, cols], preferred_element_type=F32)
            out_ref[zr, s] = acc.astype(BF)


def split_sum(value):
    high = up(value.astype(BF))
    row = lax.broadcasted_iota(jnp.int32, (16, value.shape[1]), 0)
    return jnp.where(row == 0, high, jnp.where(row == 1, value - high, 0.0)).astype(BF)


def rs_second_body(ids, w_ref, g_ref, recv_ref, rider_ref, *out_refs):
    zh, y, c = ids[0], ids[1], ids[2]
    grads = [g_ref[p].T for p in range(g_ref.shape[0])]
    for s in (1, 3, 2, 0):
        for zr, z in ((1, 1 - zh), (0, zh)):
            slot = z * 8 + lax.rem(y + s, 4) * 2 + c
            cols = pl.ds(pl.multiple_of(slot * 256, 256), 256)
            acc = up(recv_ref[zr, s])
            for p in range(len(grads)):
                acc += jnp.dot(grads[p], w_ref[p, :, cols], preferred_element_type=F32)
            out_refs[s][zr * 256 : zr * 256 + 256, :] = acc.astype(BF)
        if rider_ref.shape[0] == 1:
            out_refs[s][512:, :] = split_sum(rider_ref[...])
        else:
            out_refs[s][512:, :] = rider_ref[...]


def combine_body(p0, p1, p2, p3, near_ref, far_ref, rider_ref):
    parts = (p0, p1, p2, p3)

    def total(rows):
        return up(p0[rows, :]) + up(p1[rows, :]) + up(p2[rows, :]) + up(p3[rows, :])

    near_ref[...] = total(slice(0, 256)).astype(BF)
    far_ref[:256, :] = total(slice(256, 512)).astype(BF)
    if rider_ref.shape[0] == 1:
        row = jnp.sum(total(slice(512, 528)), axis=0, keepdims=True)
        rider_ref[...] = row
        far_ref[256:, :] = split_sum(row)
    else:
        for s, part in enumerate(parts):
            rider_ref[s] = part[512:, :]


def swap_products(ids, weight, grads, name):
    planes = grads.shape[0]
    first = call(
        rs_first_body, shape(2, 4, 256, 256), ids, weight, grads,
        flops=2 * 2048 * 256 * 256 * planes, moved=planes * 2**20, name=name + "_a",
    )
    return lax.ppermute(first, "core", SWAP)


def reduce_scatter_tp(ids, weight, grads, recv, rider, name):
    planes = grads.shape[0]
    summed = rider.shape[0] == 1
    rows = 528 if summed else 768
    blocks = call(
        rs_second_body, [shape(rows, 256)] * 4, ids, weight, grads, recv, rider,
        flops=2 * 2048 * 256 * 256 * planes, moved=planes * 2**20, name=name + "_b",
    )
    parts = [blocks[0]] + [lax.ppermute(blocks[s], "y", ring(4, s)) for s in (1, 2, 3)]
    near, far, riders = call(
        combine_body,
        [
            shape(256, 256), shape(272 if summed else 256, 256),
            shape(1, 256, dtype=F32) if summed else shape(4, 256, 256),
        ],
        *parts, smem=False, name=name + "_sum",
    )
    return blocks[0], near, lax.ppermute(far, "zh", SWAP), riders


def gather_tp(block):
    near = [block] + [lax.ppermute(block, "y", ring(4, s)) for s in (1, 2, 3)]
    other = lax.ppermute(block, "zh", SWAP)
    far = [other] + [lax.ppermute(other, "y", ring(4, s)) for s in (1, 2, 3)]
    near = jnp.stack(near)
    far = jnp.stack(far)
    return near, far, lax.ppermute(near, "core", SWAP), lax.ppermute(far, "core", SWAP)


def mixed_grad_body(near_ref, far_ref, proj_ref, mg_ref, cg_ref, head_ref):
    grads = (up(near_ref[...]) + up(far_ref[...])).T.astype(BF)
    mg_ref[...] = grads
    cg = (up(grads) * up(proj_ref[0])).astype(BF)
    cg_ref[...] = cg
    head_ref[...] = cg[:, :128]


def hidden_grad_body(near_ref, far_ref, hid_ref, og_ref, gain_ref, rms_ref, mom_ref, out_ref):
    grads = (up(near_ref[...]) + up(far_ref[:256, :])).T
    rms = rms_ref[...]
    total = mom_ref[...] + jnp.sum(up(far_ref[256:, :]), axis=0, keepdims=True)
    moment = total / (rms * 4096.0)
    out = up(og_ref[...]) + rms * (
        gain_ref[...] * grads - up(hid_ref[...]) * (rms * rms * moment)
    )
    out_ref[...] = out.astype(BF)


def out_body(ids, w_ref, hid_ref, og_ref, a_ref, b_ref, c_ref, d_ref, out_ref, send_ref, full_ref):
    for part, slots in zip((a_ref, b_ref, c_ref, d_ref), piece_slots(ids)):
        for s in range(4):
            full_ref[slots[s]] = part[s]
    mixed = full_ref[...].reshape(4096, 256)
    acc = jnp.dot(w_ref[...], mixed, preferred_element_type=F32)
    out_ref[...] = (up(hid_ref[...]) + acc).astype(BF)
    for dest in range(4):
        for k in range(2):
            send_ref[dest, k] = full_ref[(2 * ids[2] + k) * 4 + dest]
        send_ref[dest, 2] = og_ref[...]


def weight_grad_body(relative, first, ids, mine_ref, other_ref, g_ref, out_ref):
    c, x = ids[2], ids[3]
    planes = out_ref.shape[1]
    for core, ref in ((c, mine_ref), (1 - c, other_ref)):
        for k in range(2):
            acc = None
            for s in range(4):
                at = lax.rem(x + 4 - s, 4) if relative else s
                left = g_ref[at, first : first + planes].reshape(planes * 256, 256)
                term = dot_nt(left, ref[s, k])
                acc = term if acc is None else acc + term
            out_ref[2 * core + k] = acc.astype(BF).reshape(planes, 256, 256)


def weight_grads(ids, mine, other, grads, relative, first, planes, name):
    return call(
        functools.partial(weight_grad_body, relative, first), shape(4, planes, 256, 256),
        ids, mine, other, grads,
        flops=2 * 1024 * 1024 * 256 * planes, moved=planes * 2**20, name=name,
    )


def per_device(hidden_in, norm_gain, in_weight, filters, out_weight, out_grads):
    zl, x, zh, y, c = (lax.axis_index(name) for name in ("zl", "x", "zh", "y", "core"))
    ids = jnp.stack([zh, y, c, x, zl]).astype(jnp.int32)
    gain = norm_gain.reshape(16, 256)
    tp = zh * 8 + y * 2 + c
    gain_rows = lax.dynamic_slice_in_dim(norm_gain, tp * 256, 256, 0).reshape(256, 1)

    near = jnp.stack([hidden_in] + [lax.ppermute(hidden_in, "y", ring(4, s)) for s in (1, 2, 3)])
    near_swap = lax.ppermute(near, "core", SWAP)
    other = lax.ppermute(hidden_in, "zh", SWAP)
    fwd, back = call(
        toeplitz_body, [shape(16, 256, 128), shape(16, 128, 256)], after(filters, near), smem=False, name="taps"
    )
    og = out_grads[None]
    swapped = swap_products(ids, out_weight[None], og, "mixed_grads")
    _, *mg_parts, far = reduce_scatter_tp(
        ids, out_weight[None], og, swapped, after(other, near), "mixed_grads"
    )
    gathered = near, far, near_swap, lax.ppermute(far, "core", SWAP)
    proj, mixed_in, tail, rms, *send = call(
        project_body,
        [
            shape(3, 256, 256), shape(256, 256), shape(256, 128), shape(1, 256, dtype=F32),
            *[shape(2, 256, 256)] * 4,
        ],
        after(ids, mg_parts[0]), gain, in_weight, *gathered,
        scratch=[pltpu.VMEM((16, 256, 256), BF)],
        flops=2 * 768 * 4096 * 256, moved=10 * 2**20, name="project",
    )
    halo = lax.ppermute(tail, ("zl", "x"), [(i, i + 1) for i in range(15)])
    mg, cg, head = call(
        mixed_grad_body, [shape(256, 256)] * 2 + [shape(256, 128)], *mg_parts, proj,
        smem=False, name="mixed_grad",
    )
    next_halo = lax.ppermute(head, ("zl", "x"), [(i + 1, i) for i in range(15)])
    conv, mixed = call(
        conv_body, [shape(256, 256)] * 2, mixed_in, after(halo, mg_parts[1]), fwd, proj, smem=False,
        flops=2 * 256 * 256 * 256, name="conv",
    )
    pg, pg_all, part = call(
        conv_back_body,
        [shape(3, 256, 256), shape(4, 3, 256, 256), shape(1, 256, dtype=F32)],
        cg, next_halo, back, proj, conv, mg, smem=False,
        scratch=[pltpu.VMEM((256, 256), BF)], flops=2 * 256 * 256 * 256, name="conv_back",
    )
    mixed_pieces = gather_tp(after(mixed, pg))
    send = [send[0]] + [after(block, pg) for block in send[1:]]
    normed_x = [send[0]] + [lax.ppermute(send[s], "x", ring(4, s)) for s in (1, 2, 3)]
    normed_x = jnp.stack([after(normed_x[0], pg, *mixed_pieces[:2])] + normed_x[1:])
    normed_other = lax.ppermute(normed_x, "core", SWAP)
    pg_x = lax.all_to_all(pg_all, "x", 0, 0, tiled=True)
    swapped = swap_products(ids, in_weight, after(pg, normed_x), "norm_grads")
    part = part + lax.ppermute(part, "core", SWAP)
    ng_block, *ng_parts = reduce_scatter_tp(
        ids, in_weight, pg, swapped, part, "norm_grads"
    )
    in_part = weight_grads(
        ids, normed_x, normed_other, after(pg_x, mixed_pieces[0], ng_block), True, 0, 3, "in_w"
    )
    in_weight_grads = lax.psum_scatter(in_part, "zl", scatter_dimension=0, tiled=False).astype(F32)

    layer_out, m_send = call(
        out_body, [shape(256, 256), shape(4, 3, 256, 256)],
        ids, after(out_weight, in_part), hidden_in, out_grads, *mixed_pieces,
        scratch=[pltpu.VMEM((16, 256, 256), BF)],
        flops=2 * 256 * 4096 * 256, moved=4 * 2**20, name="layer_out",
    )
    taps = call(
        filter_grad_body, shape(16, 128, dtype=F32), mixed_in, halo, after(cg, m_send),
        smem=False, flops=2 * 256 * 256 * 256, name="tap_grads",
    )
    taps = taps.reshape(4, 4, 128)
    pick = lambda s: lax.dynamic_index_in_dim(taps, lax.rem(x + s, 4), 1, False)
    taps = pick(0) + sum(lax.ppermute(pick(s), "x", ring(4, s)) for s in (1, 2, 3))
    mixed_x = lax.all_to_all(m_send, "x", 0, 0, tiled=True)
    mixed_other = lax.ppermute(after(mixed_x, taps, ng_parts[1]), "core", SWAP)
    out_part = weight_grads(ids, mixed_x, mixed_other, mixed_x, False, 2, 1, "out_w")
    out_recv = lax.all_to_all(out_part[:, 0], "zl", 0, 0, tiled=True)
    out_weight_grads = jnp.sum(up(out_recv), axis=0)

    hidden_grads = call(
        hidden_grad_body, shape(256, 256), *ng_parts[:2], hidden_in, out_grads, gain_rows, rms, ng_parts[2],
        smem=False, name="hidden_grads",
    )

    row = lambda s: lax.dynamic_index_in_dim(taps, lax.rem(zl + s, 4), 0, True)
    filter_grads = row(0) + sum(lax.ppermute(row(s), "zl", ring(4, s)) for s in (1, 2, 3))

    return layer_out, hidden_grads, in_weight_grads, filter_grads, out_weight_grads


def solution(mesh):
    fine = Mesh(mesh.devices.reshape(4, 4, 2, 4, 2), ("zl", "x", "zh", "y", "core"))
    tp, ctx = ("zh", "y", "core"), ("zl", "x")
    return jax.shard_map(
        per_device,
        mesh=fine,
        in_specs=(P(tp, ctx), P(), P(None, tp, None), P(tp, None), P(tp, None), P(tp, ctx)),
        out_specs=(P(tp, ctx), P(tp, ctx), P(None, tp, ctx), P(tp + ctx, None), P(tp, ctx)),
        check_vma=False,
    )
```

```python
import functools

import jax
import jax.numpy as jnp
from jax import lax
from jax.experimental import pallas as pl
from jax.experimental.pallas import tpu as pltpu
from jax.sharding import Mesh, PartitionSpec as P

GS = 16
EPS = 1e-06
F32 = jnp.float32
BF = jnp.bfloat16
VM = pl.BlockSpec(memory_space=pltpu.VMEM)
SM = pl.BlockSpec(memory_space=pltpu.SMEM)
SWAP = [(0, 1), (1, 0)]


def shape(*dims, dtype=BF):
    return jax.ShapeDtypeStruct(dims, dtype)


def call(body, outs, *args, scratch=(), flops=0, moved=0, smem=True, name=None, limit=10):
    specs = [SM if smem and i == 0 else VM for i in range(len(args))]
    multi = isinstance(outs, (list, tuple))
    return pl.pallas_call(
        body,
        out_shape=list(outs) if multi else outs,
        in_specs=specs,
        out_specs=[VM] * len(outs) if multi else VM,
        scratch_shapes=list(scratch),
        compiler_params=pltpu.CompilerParams(vmem_limit_bytes=limit * 2**20),
        cost_estimate=pl.CostEstimate(flops=flops, bytes_accessed=moved, transcendentals=0),
        name=name,
    )(*args)


def ring(size, step):
    return [(i, (i + step) % size) for i in range(size)]


def after(value, *earlier):
    return lax.optimization_barrier((value, *earlier))[0]


def dot_nt(a, b):
    return lax.dot_general(a, b, (((1,), (1,)), ((), ())), preferred_element_type=F32)


def dot_tn(a, b):
    return lax.dot_general(a, b, (((0,), (0,)), ((), ())), preferred_element_type=F32)


def up(x):
    return x.astype(F32)


def toeplitz_body(filt_ref, fwd_ref, back_ref):
    n = filt_ref.shape[1]
    row = lax.broadcasted_iota(jnp.int32, (n, n), 0)
    col = lax.broadcasted_iota(jnp.int32, (n, n), 1)

    def group(g, _):
        mat = jnp.broadcast_to(filt_ref[pl.ds(g, 1), :], (n, n))
        step = 1
        while step < n:
            mat = jnp.where((row & step) != 0, pltpu.roll(mat, step, 1), mat)
            step *= 2
        same = jnp.where(col >= row, mat, 0.0).astype(BF)
        prev = jnp.where(col < row, mat, 0.0).astype(BF)
        fwd_ref[g, :n, :] = prev
        fwd_ref[g, n:, :] = same
        back_ref[g, :, :n] = same
        back_ref[g, :, n:] = prev
        return 0

    lax.fori_loop(0, filt_ref.shape[0], group, 0, unroll=8)


def piece_slots(ids):
    zh, y, c = ids[0], ids[1], ids[2]
    return [
        [z * 8 + lax.rem(y + 4 - s, 4) * 2 + k for s in range(4)]
        for z, k in ((zh, c), (1 - zh, c), (zh, 1 - c), (1 - zh, 1 - c))
    ]


def send_rows(ids, full_ref, send_refs):
    c, x = ids[2], ids[3]
    for s, send_ref in enumerate(send_refs):
        for k in range(2):
            send_ref[k] = full_ref[(2 * c + k) * 4 + lax.rem(x + s, 4)]


def project_body(
    ids, gain_ref, w_ref, a_ref, b_ref, c_ref, d_ref,
    proj_ref, mixed_in_ref, tail_ref, rms_ref, s0, s1, s2, s3, full_ref,
):
    parts = (a_ref, b_ref, c_ref, d_ref)
    total = jnp.zeros((1, 256), F32)
    for part in parts:
        for s in range(4):
            h = up(part[s])
            total = total + jnp.sum(h * h, axis=0, keepdims=True)
    rms = lax.rsqrt(total * (1.0 / 4096.0) + EPS)
    rms_ref[...] = rms
    gains = jnp.concatenate([gain_ref[...], jnp.zeros((112, 256), F32)], axis=0).T
    lane = lax.broadcasted_iota(jnp.int32, (256, 128), 1)
    for part, slots in zip(parts, piece_slots(ids)):
        for s in range(4):
            gain = jnp.sum(jnp.where(lane == slots[s], gains, 0.0), axis=1, keepdims=True)
            full_ref[slots[s]] = (up(part[s]) * rms * gain).astype(BF)

    normed = full_ref[...].reshape(4096, 256)
    for p in range(3):
        proj_ref[p] = jnp.dot(w_ref[p], normed, preferred_element_type=F32).astype(BF)
    mixed = (up(proj_ref[1]) * up(proj_ref[2])).astype(BF)
    mixed_in_ref[...] = mixed
    tail_ref[...] = mixed[:, 128:]
    send_rows(ids, full_ref, (s0, s1, s2, s3))


def conv_body(x_ref, halo_ref, fwd_ref, proj_ref, conv_ref, mixed_ref):
    def group(g, _):
        rows = pl.ds(pl.multiple_of(g * GS, GS), GS)
        first = jnp.concatenate([halo_ref[rows, :], x_ref[rows, :128]], axis=1)
        both = jnp.concatenate([first, x_ref[rows, :]], axis=0)
        out = jnp.dot(both, fwd_ref[g], preferred_element_type=F32).astype(BF)
        conv = jnp.concatenate([out[:GS], out[GS:]], axis=1)
        conv_ref[rows, :] = conv
        mixed_ref[rows, :] = (up(proj_ref[0, rows, :]) * up(conv)).astype(BF)
        return 0

    lax.fori_loop(0, 16, group, 0, unroll=4)


def conv_back_body(
    g_ref, halo_ref, back_ref, proj_ref, conv_ref, mg_ref, pg_ref, all_ref, part_ref, mig_ref
):
    def group(g, _):
        rows = pl.ds(pl.multiple_of(g * GS, GS), GS)
        second = jnp.concatenate([g_ref[rows, 128:], halo_ref[rows, :]], axis=1)
        both = jnp.concatenate([g_ref[rows, :], second], axis=0)
        out = dot_nt(both, back_ref[g]).astype(BF)
        mig_ref[rows, :] = jnp.concatenate([out[:GS], out[GS:]], axis=1)
        return 0

    lax.fori_loop(0, 16, group, 0, unroll=4)
    mig = up(mig_ref[...])
    key, value = up(proj_ref[1]), up(proj_ref[2])
    qg = (up(mg_ref[...]) * up(conv_ref[...])).astype(BF)
    kg = (mig * value).astype(BF)
    vg = (mig * key).astype(BF)
    pg_ref[0] = qg
    pg_ref[1] = kg
    pg_ref[2] = vg
    for dest in range(4):
        all_ref[dest] = pg_ref[...]
    terms = up(qg) * up(proj_ref[0]) + up(kg) * key + up(vg) * value
    part_ref[...] = jnp.sum(terms, axis=0, keepdims=True)


def filter_grad_body(x_ref, halo_ref, g_ref, out_ref):
    n = 128
    row = lax.broadcasted_iota(jnp.int32, (n, n), 0)
    col = lax.broadcasted_iota(jnp.int32, (n, n), 1)

    def group(g, _):
        rows = pl.ds(pl.multiple_of(g * GS, GS), GS)
        first, second = x_ref[rows, :n], x_ref[rows, n:]
        grads = jnp.concatenate([g_ref[rows, :n], g_ref[rows, n:]], axis=0)
        here = jnp.concatenate([first, second], axis=0)
        before = jnp.concatenate([halo_ref[rows, :], first], axis=0)
        mat = jnp.where(col >= row, dot_tn(here, grads), dot_tn(before, grads))
        step = 1
        while step < n:
            mat = jnp.where((row & step) != 0, pltpu.roll(mat, n - step, 1), mat)
            step *= 2
        out_ref[pl.ds(g, 1), :] = jnp.sum(mat, axis=0, keepdims=True)
        return 0

    lax.fori_loop(0, 16, group, 0, unroll=8)


def rs_first_body(ids, w_ref, g_ref, out_ref):
    zh, y, c = ids[0], ids[1], ids[2]
    grads = [g_ref[p].T for p in range(g_ref.shape[0])]
    for zr, z in enumerate((zh, 1 - zh)):
        for s in range(4):
            slot = z * 8 + lax.rem(y + s, 4) * 2 + (1 - c)
            cols = pl.ds(pl.multiple_of(slot * 256, 256), 256)
            acc = jnp.dot(grads[0], w_ref[0, :, cols], preferred_element_type=F32)
            for p in range(1, len(grads)):
                acc += jnp.dot(grads[p], w_ref[p, :, cols], preferred_element_type=F32)
            out_ref[zr, s] = acc.astype(BF)


def split_sum(value):
    high = up(value.astype(BF))
    row = lax.broadcasted_iota(jnp.int32, (16, value.shape[1]), 0)
    return jnp.where(row == 0, high, jnp.where(row == 1, value - high, 0.0)).astype(BF)


def rs_second_body(ids, w_ref, g_ref, recv_ref, rider_ref, *out_refs):
    zh, y, c = ids[0], ids[1], ids[2]
    grads = [g_ref[p].T for p in range(g_ref.shape[0])]
    for s in (1, 3, 2, 0):
        for zr, z in ((1, 1 - zh), (0, zh)):
            slot = z * 8 + lax.rem(y + s, 4) * 2 + c
            cols = pl.ds(pl.multiple_of(slot * 256, 256), 256)
            acc = up(recv_ref[zr, s])
            for p in range(len(grads)):
                acc += jnp.dot(grads[p], w_ref[p, :, cols], preferred_element_type=F32)
            out_refs[s][zr * 256 : zr * 256 + 256, :] = acc.astype(BF)
        if rider_ref.shape[0] == 1:
            out_refs[s][512:, :] = split_sum(rider_ref[...])
        else:
            out_refs[s][512:, :] = rider_ref[...]


def combine_body(p0, p1, p2, p3, near_ref, far_ref, rider_ref):
    parts = (p0, p1, p2, p3)

    def total(rows):
        return up(p0[rows, :]) + up(p1[rows, :]) + up(p2[rows, :]) + up(p3[rows, :])

    near_ref[...] = total(slice(0, 256)).astype(BF)
    far_ref[:256, :] = total(slice(256, 512)).astype(BF)
    if rider_ref.shape[0] == 1:
        row = jnp.sum(total(slice(512, 528)), axis=0, keepdims=True)
        rider_ref[...] = row
        far_ref[256:, :] = split_sum(row)
    else:
        for s, part in enumerate(parts):
            rider_ref[s] = part[512:, :]


def swap_products(ids, weight, grads, name):
    planes = grads.shape[0]
    first = call(
        rs_first_body, shape(2, 4, 256, 256), ids, weight, grads,
        flops=2 * 2048 * 256 * 256 * planes, moved=planes * 2**20, name=name + "_a",
    )
    return lax.ppermute(first, "core", SWAP)


def reduce_scatter_tp(ids, weight, grads, recv, rider, name):
    planes = grads.shape[0]
    summed = rider.shape[0] == 1
    rows = 528 if summed else 768
    blocks = call(
        rs_second_body, [shape(rows, 256)] * 4, ids, weight, grads, recv, rider,
        flops=2 * 2048 * 256 * 256 * planes, moved=planes * 2**20, name=name + "_b",
    )
    parts = [blocks[0]] + [lax.ppermute(blocks[s], "y", ring(4, s)) for s in (1, 2, 3)]
    near, far, riders = call(
        combine_body,
        [
            shape(256, 256), shape(272 if summed else 256, 256),
            shape(1, 256, dtype=F32) if summed else shape(4, 256, 256),
        ],
        *parts, smem=False, name=name + "_sum",
    )
    return blocks[0], near, lax.ppermute(far, "zh", SWAP), riders


def gather_tp(block):
    near = [block] + [lax.ppermute(block, "y", ring(4, s)) for s in (1, 2, 3)]
    other = lax.ppermute(block, "zh", SWAP)
    far = [other] + [lax.ppermute(other, "y", ring(4, s)) for s in (1, 2, 3)]
    near = jnp.stack(near)
    far = jnp.stack(far)
    return near, far, lax.ppermute(near, "core", SWAP), lax.ppermute(far, "core", SWAP)


def mixed_grad_body(near_ref, far_ref, proj_ref, mg_ref, cg_ref, head_ref):
    grads = (up(near_ref[...]) + up(far_ref[...])).T.astype(BF)
    mg_ref[...] = grads
    cg = (up(grads) * up(proj_ref[0])).astype(BF)
    cg_ref[...] = cg
    head_ref[...] = cg[:, :128]


def hidden_grad_body(near_ref, far_ref, hid_ref, og_ref, gain_ref, rms_ref, mom_ref, out_ref):
    grads = (up(near_ref[...]) + up(far_ref[:256, :])).T
    rms = rms_ref[...]
    total = mom_ref[...] + jnp.sum(up(far_ref[256:, :]), axis=0, keepdims=True)
    moment = total / (rms * 4096.0)
    out = up(og_ref[...]) + rms * (
        gain_ref[...] * grads - up(hid_ref[...]) * (rms * rms * moment)
    )
    out_ref[...] = out.astype(BF)


def out_body(ids, w_ref, hid_ref, og_ref, a_ref, b_ref, c_ref, d_ref, out_ref, send_ref, full_ref):
    for part, slots in zip((a_ref, b_ref, c_ref, d_ref), piece_slots(ids)):
        for s in range(4):
            full_ref[slots[s]] = part[s]
    mixed = full_ref[...].reshape(4096, 256)
    acc = jnp.dot(w_ref[...], mixed, preferred_element_type=F32)
    out_ref[...] = (up(hid_ref[...]) + acc).astype(BF)
    for dest in range(4):
        for k in range(2):
            send_ref[dest, k] = full_ref[(2 * ids[2] + k) * 4 + dest]
        send_ref[dest, 2] = og_ref[...]


def weight_grad_body(relative, first, ids, mine_ref, other_ref, g_ref, out_ref):
    c, x = ids[2], ids[3]
    planes = out_ref.shape[1]
    for core, ref in ((c, mine_ref), (1 - c, other_ref)):
        for k in range(2):
            acc = None
            for s in range(4):
                at = lax.rem(x + 4 - s, 4) if relative else s
                left = g_ref[at, first : first + planes].reshape(planes * 256, 256)
                term = dot_nt(left, ref[s, k])
                acc = term if acc is None else acc + term
            out_ref[2 * core + k] = acc.astype(BF).reshape(planes, 256, 256)


def weight_grads(ids, mine, other, grads, relative, first, planes, name):
    return call(
        functools.partial(weight_grad_body, relative, first), shape(4, planes, 256, 256),
        ids, mine, other, grads,
        flops=2 * 1024 * 1024 * 256 * planes, moved=planes * 2**20, name=name,
    )


def per_device(hidden_in, norm_gain, in_weight, filters, out_weight, out_grads):
    zl, x, zh, y, c = (lax.axis_index(name) for name in ("zl", "x", "zh", "y", "core"))
    ids = jnp.stack([zh, y, c, x, zl]).astype(jnp.int32)
    gain = norm_gain.reshape(16, 256)
    tp = zh * 8 + y * 2 + c
    gain_rows = lax.dynamic_slice_in_dim(norm_gain, tp * 256, 256, 0).reshape(256, 1)

    near = jnp.stack([hidden_in] + [lax.ppermute(hidden_in, "y", ring(4, s)) for s in (1, 2, 3)])
    near_swap = lax.ppermute(near, "core", SWAP)
    other = lax.ppermute(hidden_in, "zh", SWAP)
    fwd, back = call(
        toeplitz_body, [shape(16, 256, 128), shape(16, 128, 256)], after(filters, near), smem=False, name="taps"
    )
    og = out_grads[None]
    swapped = swap_products(ids, out_weight[None], og, "mixed_grads")
    _, *mg_parts, far = reduce_scatter_tp(
        ids, out_weight[None], og, swapped, after(other, near), "mixed_grads"
    )
    gathered = near, far, near_swap, lax.ppermute(far, "core", SWAP)
    proj, mixed_in, tail, rms, *send = call(
        project_body,
        [
            shape(3, 256, 256), shape(256, 256), shape(256, 128), shape(1, 256, dtype=F32),
            *[shape(2, 256, 256)] * 4,
        ],
        after(ids, mg_parts[0]), gain, in_weight, *gathered,
        scratch=[pltpu.VMEM((16, 256, 256), BF)],
        flops=2 * 768 * 4096 * 256, moved=10 * 2**20, name="project",
    )
    halo = lax.ppermute(tail, ("zl", "x"), [(i, i + 1) for i in range(15)])
    mg, cg, head = call(
        mixed_grad_body, [shape(256, 256)] * 2 + [shape(256, 128)], *mg_parts, proj,
        smem=False, name="mixed_grad",
    )
    next_halo = lax.ppermute(head, ("zl", "x"), [(i + 1, i) for i in range(15)])
    conv, mixed = call(
        conv_body, [shape(256, 256)] * 2, mixed_in, after(halo, mg_parts[1]), fwd, proj, smem=False,
        flops=2 * 256 * 256 * 256, name="conv",
    )
    pg, pg_all, part = call(
        conv_back_body,
        [shape(3, 256, 256), shape(4, 3, 256, 256), shape(1, 256, dtype=F32)],
        cg, next_halo, back, proj, conv, mg, smem=False,
        scratch=[pltpu.VMEM((256, 256), BF)], flops=2 * 256 * 256 * 256, name="conv_back",
    )
    mixed_pieces = gather_tp(after(mixed, pg))
    send = [send[0]] + [after(block, pg) for block in send[1:]]
    normed_x = [send[0]] + [lax.ppermute(send[s], "x", ring(4, s)) for s in (1, 2, 3)]
    normed_x = jnp.stack([after(normed_x[0], pg, *mixed_pieces[:2])] + normed_x[1:])
    normed_other = lax.ppermute(normed_x, "core", SWAP)
    pg_x = lax.all_to_all(pg_all, "x", 0, 0, tiled=True)
    swapped = swap_products(ids, in_weight, after(pg, normed_x), "norm_grads")
    part = part + lax.ppermute(part, "core", SWAP)
    ng_block, *ng_parts = reduce_scatter_tp(
        ids, in_weight, pg, swapped, part, "norm_grads"
    )
    layer_out, m_send = call(
        out_body, [shape(256, 256), shape(4, 3, 256, 256)],
        ids, out_weight, hidden_in, out_grads, *mixed_pieces,
        scratch=[pltpu.VMEM((16, 256, 256), BF)],
        flops=2 * 256 * 4096 * 256, moved=4 * 2**20, name="layer_out",
    )
    in_part = weight_grads(
        ids, normed_x, normed_other, after(pg_x, m_send, ng_block), True, 0, 3, "in_w"
    )
    in_weight_grads = lax.psum_scatter(in_part, "zl", scatter_dimension=0, tiled=False).astype(F32)

    taps = call(
        filter_grad_body, shape(16, 128, dtype=F32), mixed_in, halo, after(cg, in_part),
        smem=False, flops=2 * 256 * 256 * 256, name="tap_grads",
    )
    taps = taps.reshape(4, 4, 128)
    pick = lambda s: lax.dynamic_index_in_dim(taps, lax.rem(x + s, 4), 1, False)
    taps = pick(0) + sum(lax.ppermute(pick(s), "x", ring(4, s)) for s in (1, 2, 3))
    mixed_x = lax.all_to_all(after(m_send, pg_x), "x", 0, 0, tiled=True)
    mixed_other = lax.ppermute(after(mixed_x, taps, ng_parts[0]), "core", SWAP)
    out_part = weight_grads(ids, mixed_x, mixed_other, mixed_x, False, 2, 1, "out_w")
    out_recv = lax.all_to_all(out_part[:, 0], "zl", 0, 0, tiled=True)
    out_weight_grads = jnp.sum(up(out_recv), axis=0)

    hidden_grads = call(
        hidden_grad_body, shape(256, 256), *ng_parts[:2], hidden_in, out_grads, gain_rows, rms, ng_parts[2],
        smem=False, name="hidden_grads",
    )

    row = lambda s: lax.dynamic_index_in_dim(taps, lax.rem(zl + s, 4), 0, True)
    filter_grads = row(0) + sum(lax.ppermute(row(s), "zl", ring(4, s)) for s in (1, 2, 3))

    return layer_out, hidden_grads, in_weight_grads, filter_grads, out_weight_grads


def solution(mesh):
    fine = Mesh(mesh.devices.reshape(4, 4, 2, 4, 2), ("zl", "x", "zh", "y", "core"))
    tp, ctx = ("zh", "y", "core"), ("zl", "x")
    return jax.shard_map(
        per_device,
        mesh=fine,
        in_specs=(P(tp, ctx), P(), P(None, tp, None), P(tp, None), P(tp, None), P(tp, ctx)),
        out_specs=(P(tp, ctx), P(tp, ctx), P(None, tp, ctx), P(tp + ctx, None), P(tp, ctx)),
        check_vma=False,
    )
```

```python
import functools

import jax
import jax.numpy as jnp
from jax import lax
from jax.experimental import pallas as pl
from jax.experimental.pallas import tpu as pltpu
from jax.sharding import Mesh, PartitionSpec as P

GS = 16
EPS = 1e-06
F32 = jnp.float32
BF = jnp.bfloat16
VM = pl.BlockSpec(memory_space=pltpu.VMEM)
SM = pl.BlockSpec(memory_space=pltpu.SMEM)
SWAP = [(0, 1), (1, 0)]


def shape(*dims, dtype=BF):
    return jax.ShapeDtypeStruct(dims, dtype)


def call(body, outs, *args, scratch=(), flops=0, moved=0, smem=True, name=None, limit=10):
    specs = [SM if smem and i == 0 else VM for i in range(len(args))]
    multi = isinstance(outs, (list, tuple))
    return pl.pallas_call(
        body,
        out_shape=list(outs) if multi else outs,
        in_specs=specs,
        out_specs=[VM] * len(outs) if multi else VM,
        scratch_shapes=list(scratch),
        compiler_params=pltpu.CompilerParams(vmem_limit_bytes=limit * 2**20),
        cost_estimate=pl.CostEstimate(flops=flops, bytes_accessed=moved, transcendentals=0),
        name=name,
    )(*args)


def ring(size, step):
    return [(i, (i + step) % size) for i in range(size)]


def after(value, *earlier):
    return lax.optimization_barrier((value, *earlier))[0]


def dot_nt(a, b):
    return lax.dot_general(a, b, (((1,), (1,)), ((), ())), preferred_element_type=F32)


def dot_tn(a, b):
    return lax.dot_general(a, b, (((0,), (0,)), ((), ())), preferred_element_type=F32)


def up(x):
    return x.astype(F32)


def toeplitz_body(filt_ref, fwd_ref, back_ref):
    n = filt_ref.shape[1]
    row = lax.broadcasted_iota(jnp.int32, (n, n), 0)
    col = lax.broadcasted_iota(jnp.int32, (n, n), 1)

    def group(g, _):
        mat = jnp.broadcast_to(filt_ref[pl.ds(g, 1), :], (n, n))
        step = 1
        while step < n:
            mat = jnp.where((row & step) != 0, pltpu.roll(mat, step, 1), mat)
            step *= 2
        same = jnp.where(col >= row, mat, 0.0).astype(BF)
        prev = jnp.where(col < row, mat, 0.0).astype(BF)
        fwd_ref[g, :n, :] = prev
        fwd_ref[g, n:, :] = same
        back_ref[g, :, :n] = same
        back_ref[g, :, n:] = prev
        return 0

    lax.fori_loop(0, filt_ref.shape[0], group, 0, unroll=8)


def piece_slots(ids):
    zh, y, c = ids[0], ids[1], ids[2]
    return [
        [z * 8 + lax.rem(y + 4 - s, 4) * 2 + k for s in range(4)]
        for z, k in ((zh, c), (1 - zh, c), (zh, 1 - c), (1 - zh, 1 - c))
    ]


def send_rows(ids, full_ref, send_refs):
    c, x = ids[2], ids[3]
    for s, send_ref in enumerate(send_refs):
        for k in range(2):
            send_ref[k] = full_ref[(2 * c + k) * 4 + lax.rem(x + s, 4)]


def project_body(
    ids, gain_ref, w_ref, a_ref, b_ref, c_ref, d_ref,
    proj_ref, mixed_in_ref, tail_ref, rms_ref, s0, s1, s2, s3, full_ref,
):
    parts = (a_ref, b_ref, c_ref, d_ref)
    total = jnp.zeros((1, 256), F32)
    for part in parts:
        for s in range(4):
            h = up(part[s])
            total = total + jnp.sum(h * h, axis=0, keepdims=True)
    rms = lax.rsqrt(total * (1.0 / 4096.0) + EPS)
    rms_ref[...] = rms
    gains = jnp.concatenate([gain_ref[...], jnp.zeros((112, 256), F32)], axis=0).T
    lane = lax.broadcasted_iota(jnp.int32, (256, 128), 1)
    for part, slots in zip(parts, piece_slots(ids)):
        for s in range(4):
            gain = jnp.sum(jnp.where(lane == slots[s], gains, 0.0), axis=1, keepdims=True)
            full_ref[slots[s]] = (up(part[s]) * rms * gain).astype(BF)

    normed = full_ref[...].reshape(4096, 256)
    for p in range(3):
        proj_ref[p] = jnp.dot(w_ref[p], normed, preferred_element_type=F32).astype(BF)
    mixed = (up(proj_ref[1]) * up(proj_ref[2])).astype(BF)
    mixed_in_ref[...] = mixed
    tail_ref[...] = mixed[:, 128:]
    send_rows(ids, full_ref, (s0, s1, s2, s3))


def conv_body(x_ref, halo_ref, fwd_ref, proj_ref, conv_ref, mixed_ref):
    def group(g, _):
        rows = pl.ds(pl.multiple_of(g * GS, GS), GS)
        first = jnp.concatenate([halo_ref[rows, :], x_ref[rows, :128]], axis=1)
        both = jnp.concatenate([first, x_ref[rows, :]], axis=0)
        out = jnp.dot(both, fwd_ref[g], preferred_element_type=F32).astype(BF)
        conv = jnp.concatenate([out[:GS], out[GS:]], axis=1)
        conv_ref[rows, :] = conv
        mixed_ref[rows, :] = (up(proj_ref[0, rows, :]) * up(conv)).astype(BF)
        return 0

    lax.fori_loop(0, 16, group, 0, unroll=4)


def conv_back_body(
    g_ref, halo_ref, back_ref, proj_ref, conv_ref, mg_ref, pg_ref, all_ref, part_ref, mig_ref
):
    def group(g, _):
        rows = pl.ds(pl.multiple_of(g * GS, GS), GS)
        second = jnp.concatenate([g_ref[rows, 128:], halo_ref[rows, :]], axis=1)
        both = jnp.concatenate([g_ref[rows, :], second], axis=0)
        out = dot_nt(both, back_ref[g]).astype(BF)
        mig_ref[rows, :] = jnp.concatenate([out[:GS], out[GS:]], axis=1)
        return 0

    lax.fori_loop(0, 16, group, 0, unroll=4)
    mig = up(mig_ref[...])
    key, value = up(proj_ref[1]), up(proj_ref[2])
    qg = (up(mg_ref[...]) * up(conv_ref[...])).astype(BF)
    kg = (mig * value).astype(BF)
    vg = (mig * key).astype(BF)
    pg_ref[0] = qg
    pg_ref[1] = kg
    pg_ref[2] = vg
    for dest in range(4):
        all_ref[dest] = pg_ref[...]
    terms = up(qg) * up(proj_ref[0]) + up(kg) * key + up(vg) * value
    part_ref[...] = jnp.sum(terms, axis=0, keepdims=True)


def filter_grad_body(x_ref, halo_ref, g_ref, out_ref):
    n = 128
    row = lax.broadcasted_iota(jnp.int32, (n, n), 0)
    col = lax.broadcasted_iota(jnp.int32, (n, n), 1)

    def group(g, _):
        rows = pl.ds(pl.multiple_of(g * GS, GS), GS)
        first, second = x_ref[rows, :n], x_ref[rows, n:]
        grads = jnp.concatenate([g_ref[rows, :n], g_ref[rows, n:]], axis=0)
        here = jnp.concatenate([first, second], axis=0)
        before = jnp.concatenate([halo_ref[rows, :], first], axis=0)
        mat = jnp.where(col >= row, dot_tn(here, grads), dot_tn(before, grads))
        step = 1
        while step < n:
            mat = jnp.where((row & step) != 0, pltpu.roll(mat, n - step, 1), mat)
            step *= 2
        out_ref[pl.ds(g, 1), :] = jnp.sum(mat, axis=0, keepdims=True)
        return 0

    lax.fori_loop(0, 16, group, 0, unroll=8)


def rs_first_body(ids, w_ref, g_ref, out_ref):
    zh, y, c = ids[0], ids[1], ids[2]
    grads = [g_ref[p].T for p in range(g_ref.shape[0])]
    for zr, z in enumerate((zh, 1 - zh)):
        for s in range(4):
            slot = z * 8 + lax.rem(y + s, 4) * 2 + (1 - c)
            cols = pl.ds(pl.multiple_of(slot * 256, 256), 256)
            acc = jnp.dot(grads[0], w_ref[0, :, cols], preferred_element_type=F32)
            for p in range(1, len(grads)):
                acc += jnp.dot(grads[p], w_ref[p, :, cols], preferred_element_type=F32)
            out_ref[zr, s] = acc.astype(BF)


def split_sum(value):
    high = up(value.astype(BF))
    row = lax.broadcasted_iota(jnp.int32, (16, value.shape[1]), 0)
    return jnp.where(row == 0, high, jnp.where(row == 1, value - high, 0.0)).astype(BF)


def rs_second_body(ids, w_ref, g_ref, recv_ref, rider_ref, *out_refs):
    zh, y, c = ids[0], ids[1], ids[2]
    grads = [g_ref[p].T for p in range(g_ref.shape[0])]
    for s in (1, 3, 2, 0):
        for zr, z in ((1, 1 - zh), (0, zh)):
            slot = z * 8 + lax.rem(y + s, 4) * 2 + c
            cols = pl.ds(pl.multiple_of(slot * 256, 256), 256)
            acc = up(recv_ref[zr, s])
            for p in range(len(grads)):
                acc += jnp.dot(grads[p], w_ref[p, :, cols], preferred_element_type=F32)
            out_refs[s][zr * 256 : zr * 256 + 256, :] = acc.astype(BF)
        if rider_ref.shape[0] == 1:
            out_refs[s][512:, :] = split_sum(rider_ref[...])
        else:
            out_refs[s][512:, :] = rider_ref[...]


def combine_body(p0, p1, p2, p3, near_ref, far_ref, rider_ref):
    parts = (p0, p1, p2, p3)

    def total(rows):
        return up(p0[rows, :]) + up(p1[rows, :]) + up(p2[rows, :]) + up(p3[rows, :])

    near_ref[...] = total(slice(0, 256)).astype(BF)
    far_ref[:256, :] = total(slice(256, 512)).astype(BF)
    if rider_ref.shape[0] == 1:
        row = jnp.sum(total(slice(512, 528)), axis=0, keepdims=True)
        rider_ref[...] = row
        far_ref[256:, :] = split_sum(row)
    else:
        for s, part in enumerate(parts):
            rider_ref[s] = part[512:, :]


def swap_products(ids, weight, grads, name):
    planes = grads.shape[0]
    first = call(
        rs_first_body, shape(2, 4, 256, 256), ids, weight, grads,
        flops=2 * 2048 * 256 * 256 * planes, moved=planes * 2**20, name=name + "_a",
    )
    return lax.ppermute(first, "core", SWAP)


def reduce_scatter_tp(ids, weight, grads, recv, rider, name):
    planes = grads.shape[0]
    summed = rider.shape[0] == 1
    rows = 528 if summed else 768
    blocks = call(
        rs_second_body, [shape(rows, 256)] * 4, ids, weight, grads, recv, rider,
        flops=2 * 2048 * 256 * 256 * planes, moved=planes * 2**20, name=name + "_b",
    )
    parts = [blocks[0]] + [lax.ppermute(blocks[s], "y", ring(4, s)) for s in (1, 2, 3)]
    near, far, riders = call(
        combine_body,
        [
            shape(256, 256), shape(272 if summed else 256, 256),
            shape(1, 256, dtype=F32) if summed else shape(4, 256, 256),
        ],
        *parts, smem=False, name=name + "_sum",
    )
    return blocks[0], near, lax.ppermute(far, "zh", SWAP), riders


def gather_tp(block):
    near = [block] + [lax.ppermute(block, "y", ring(4, s)) for s in (1, 2, 3)]
    other = lax.ppermute(block, "zh", SWAP)
    far = [other] + [lax.ppermute(other, "y", ring(4, s)) for s in (1, 2, 3)]
    near = jnp.stack(near)
    far = jnp.stack(far)
    return near, far, lax.ppermute(near, "core", SWAP), lax.ppermute(far, "core", SWAP)


def mixed_grad_body(near_ref, far_ref, proj_ref, mg_ref, cg_ref, head_ref):
    grads = (up(near_ref[...]) + up(far_ref[...])).T.astype(BF)
    mg_ref[...] = grads
    cg = (up(grads) * up(proj_ref[0])).astype(BF)
    cg_ref[...] = cg
    head_ref[...] = cg[:, :128]


def hidden_grad_body(near_ref, far_ref, hid_ref, og_ref, gain_ref, rms_ref, mom_ref, out_ref):
    grads = (up(near_ref[...]) + up(far_ref[:256, :])).T
    rms = rms_ref[...]
    total = mom_ref[...] + jnp.sum(up(far_ref[256:, :]), axis=0, keepdims=True)
    moment = total / (rms * 4096.0)
    out = up(og_ref[...]) + rms * (
        gain_ref[...] * grads - up(hid_ref[...]) * (rms * rms * moment)
    )
    out_ref[...] = out.astype(BF)


def out_body(ids, w_ref, hid_ref, og_ref, a_ref, b_ref, c_ref, d_ref, out_ref, send_ref, full_ref):
    for part, slots in zip((a_ref, b_ref, c_ref, d_ref), piece_slots(ids)):
        for s in range(4):
            full_ref[slots[s]] = part[s]
    mixed = full_ref[...].reshape(4096, 256)
    acc = jnp.dot(w_ref[...], mixed, preferred_element_type=F32)
    out_ref[...] = (up(hid_ref[...]) + acc).astype(BF)
    for dest in range(4):
        for k in range(2):
            send_ref[dest, k] = full_ref[(2 * ids[2] + k) * 4 + dest]
        send_ref[dest, 2] = og_ref[...]


def weight_grad_body(relative, first, ids, mine_ref, other_ref, g_ref, out_ref):
    c, x = ids[2], ids[3]
    planes = out_ref.shape[1]
    for core, ref in ((c, mine_ref), (1 - c, other_ref)):
        for k in range(2):
            acc = None
            for s in range(4):
                at = lax.rem(x + 4 - s, 4) if relative else s
                left = g_ref[at, first : first + planes].reshape(planes * 256, 256)
                term = dot_nt(left, ref[s, k])
                acc = term if acc is None else acc + term
            out_ref[2 * core + k] = acc.astype(BF).reshape(planes, 256, 256)


def weight_grads(ids, mine, other, grads, relative, first, planes, name):
    return call(
        functools.partial(weight_grad_body, relative, first), shape(4, planes, 256, 256),
        ids, mine, other, grads,
        flops=2 * 1024 * 1024 * 256 * planes, moved=planes * 2**20, name=name,
    )


def per_device(hidden_in, norm_gain, in_weight, filters, out_weight, out_grads):
    zl, x, zh, y, c = (lax.axis_index(name) for name in ("zl", "x", "zh", "y", "core"))
    ids = jnp.stack([zh, y, c, x, zl]).astype(jnp.int32)
    gain = norm_gain.reshape(16, 256)
    tp = zh * 8 + y * 2 + c
    gain_rows = lax.dynamic_slice_in_dim(norm_gain, tp * 256, 256, 0).reshape(256, 1)

    near = jnp.stack([hidden_in] + [lax.ppermute(hidden_in, "y", ring(4, s)) for s in (1, 2, 3)])
    near_swap = lax.ppermute(near, "core", SWAP)
    other = lax.ppermute(hidden_in, "zh", SWAP)
    fwd, back = call(
        toeplitz_body, [shape(16, 256, 128), shape(16, 128, 256)], after(filters, near), smem=False, name="taps"
    )
    og = out_grads[None]
    swapped = swap_products(ids, out_weight[None], og, "mixed_grads")
    _, *mg_parts, far = reduce_scatter_tp(
        ids, out_weight[None], og, swapped, after(other, near), "mixed_grads"
    )
    gathered = near, far, near_swap, lax.ppermute(far, "core", SWAP)
    proj, mixed_in, tail, rms, *send = call(
        project_body,
        [
            shape(3, 256, 256), shape(256, 256), shape(256, 128), shape(1, 256, dtype=F32),
            *[shape(2, 256, 256)] * 4,
        ],
        after(ids, mg_parts[0]), gain, in_weight, *gathered,
        scratch=[pltpu.VMEM((16, 256, 256), BF)],
        flops=2 * 768 * 4096 * 256, moved=10 * 2**20, name="project",
    )
    halo = lax.ppermute(tail, ("zl", "x"), [(i, i + 1) for i in range(15)])
    mg, cg, head = call(
        mixed_grad_body, [shape(256, 256)] * 2 + [shape(256, 128)], *mg_parts, proj,
        smem=False, name="mixed_grad",
    )
    next_halo = lax.ppermute(head, ("zl", "x"), [(i + 1, i) for i in range(15)])
    conv, mixed = call(
        conv_body, [shape(256, 256)] * 2, mixed_in, after(halo, mg_parts[1]), fwd, proj, smem=False,
        flops=2 * 256 * 256 * 256, name="conv",
    )
    pg, pg_all, part = call(
        conv_back_body,
        [shape(3, 256, 256), shape(4, 3, 256, 256), shape(1, 256, dtype=F32)],
        cg, next_halo, back, proj, conv, mg, smem=False,
        scratch=[pltpu.VMEM((256, 256), BF)], flops=2 * 256 * 256 * 256, name="conv_back",
    )
    mixed_pieces = gather_tp(after(mixed, pg))
    send = [send[0]] + [after(block, pg) for block in send[1:]]
    normed_x = [send[0]] + [lax.ppermute(send[s], "x", ring(4, s)) for s in (1, 2, 3)]
    normed_x = jnp.stack([after(normed_x[0], pg, *mixed_pieces[:2])] + normed_x[1:])
    normed_other = lax.ppermute(normed_x, "core", SWAP)
    pg_x = lax.all_to_all(pg_all, "x", 0, 0, tiled=True)
    swapped = swap_products(ids, in_weight, after(pg, normed_x), "norm_grads")
    layer_out, m_send = call(
        out_body, [shape(256, 256), shape(4, 3, 256, 256)],
        ids, out_weight, hidden_in, out_grads, *mixed_pieces,
        scratch=[pltpu.VMEM((16, 256, 256), BF)],
        flops=2 * 256 * 4096 * 256, moved=4 * 2**20, name="layer_out",
    )
    in_part = weight_grads(
        ids, normed_x, normed_other, after(pg_x, m_send, swapped), True, 0, 3, "in_w"
    )
    in_weight_grads = lax.psum_scatter(in_part, "zl", scatter_dimension=0, tiled=False).astype(F32)

    part = part + lax.ppermute(part, "core", SWAP)
    ng_block, *ng_parts = reduce_scatter_tp(
        ids, in_weight, pg, after(swapped, in_part), part, "norm_grads"
    )
    taps = call(
        filter_grad_body, shape(16, 128, dtype=F32), mixed_in, halo, after(cg, in_part),
        smem=False, flops=2 * 256 * 256 * 256, name="tap_grads",
    )
    taps = taps.reshape(4, 4, 128)
    pick = lambda s: lax.dynamic_index_in_dim(taps, lax.rem(x + s, 4), 1, False)
    taps = pick(0) + sum(lax.ppermute(pick(s), "x", ring(4, s)) for s in (1, 2, 3))
    mixed_x = lax.all_to_all(after(m_send, in_part), "x", 0, 0, tiled=True)
    mixed_other = lax.ppermute(after(mixed_x, taps, ng_parts[0]), "core", SWAP)
    out_part = weight_grads(ids, mixed_x, mixed_other, mixed_x, False, 2, 1, "out_w")
    out_recv = lax.all_to_all(out_part[:, 0], "zl", 0, 0, tiled=True)
    out_weight_grads = jnp.sum(up(out_recv), axis=0)

    hidden_grads = call(
        hidden_grad_body, shape(256, 256), *ng_parts[:2], hidden_in, out_grads, gain_rows, rms, ng_parts[2],
        smem=False, name="hidden_grads",
    )

    row = lambda s: lax.dynamic_index_in_dim(taps, lax.rem(zl + s, 4), 0, True)
    filter_grads = row(0) + sum(lax.ppermute(row(s), "zl", ring(4, s)) for s in (1, 2, 3))

    return layer_out, hidden_grads, in_weight_grads, filter_grads, out_weight_grads


def solution(mesh):
    fine = Mesh(mesh.devices.reshape(4, 4, 2, 4, 2), ("zl", "x", "zh", "y", "core"))
    tp, ctx = ("zh", "y", "core"), ("zl", "x")
    return jax.shard_map(
        per_device,
        mesh=fine,
        in_specs=(P(tp, ctx), P(), P(None, tp, None), P(tp, None), P(tp, None), P(tp, ctx)),
        out_specs=(P(tp, ctx), P(tp, ctx), P(None, tp, ctx), P(tp + ctx, None), P(tp, ctx)),
        check_vma=False,
    )
```
